128 devices in a mesh: dom: 16 (over x, z_hi, core), space: 8 (over y, z_lo).
Axes of the slice: x: 4, y: 4, z: 4 (z_hi: 2, z_lo: 2; z = z_hi * 2 + z_lo), core: 2. Of those that a mesh axis runs over, the one named last changes fastest.
Arguments:
- particles: float32 [32, 3, 512, 1024], P('dom', None, 'space'), may hold values from -6 to 6
- copies: int32 [32], replicated, may hold values from 0 to 31
- depth_class: int32 [512, 1024], P('space'), may hold values from 0 to 7
- depth_table: float32 [8], replicated, may hold values from 0.5 to 2
- observed: float32 [512, 1024], P('space'), may hold values from -6 to 6
- nudge_gain: float32 [512, 1024], P('space'), may hold values from 0.02 to 0.3
Outputs:
- advanced: float32 [32, 3, 512, 1024], P('dom', None, 'space')
The draws below stay inside these ranges and needn't reach their ends.
All inputs are finite; a program needn't handle non-finite values.
Results may differ from the reference program's by a relative error of at most 0.00002.
Values sent between devices are 32-bit elements; how exact they have to be, the bound alone decides.
A program may use at most 128 MiB of HBM per device.

```python
import math
import jax
import jax.numpy as jnp
import numpy as np
from jax import lax

COLS = 1024
STEPS = 4
CLASSES = 8
PARTS_SIZE = 32
NROWS = 512


def place_ends(values, stream_key, low, largest):
    longest = values.shape.index(max(values.shape))
    spots = []
    for shift in (0, 1):
        where = [jax.random.randint(jax.random.fold_in(stream_key, axis), (), 0, length) for axis, length in enumerate(values.shape)]
        where[longest] = (where[longest] + shift) % values.shape[longest]
        spots.append(tuple(where))
    return values.at[spots[0]].set(low).at[spots[1]].set(largest)


def block_levels(rng, shape, cuts, smallest, top_value):
    def one(axis_at, shards_of):
        draws = jax.random.uniform(jax.random.fold_in(jax.random.fold_in(rng, 6), axis_at), (shards_of,), jnp.float32, smallest / len(cuts), top_value / len(cuts))
        return jnp.repeat(jnp.exp(draws), shape[axis_at] // shards_of).reshape((-1,) + (1,) * (len(shape) - axis_at - 1))

    loudness = one(*cuts[0])
    for cut in cuts[1:]:
        loudness = loudness * one(*cut)
    return loudness


def rank_table(count, slope):
    portions = [(1 << 20) // math.isqrt(grade ** slope) + 1 for grade in range(1, count + 1)]
    deviation = 1 + sum(portions) // (1 << 30)
    return np.cumsum(np.array([max(1, weight // deviation) for weight in portions]))


def ranked(own_key, extent, number_of, skew):
    table = rank_table(number_of, skew)
    pick = jax.random.randint(jax.random.fold_in(own_key, 1), extent, 0, int(table[number_of - 1]))
    grade = jnp.searchsorted(jnp.asarray(table, jnp.int32), pick, side="right")
    return jax.random.permutation(jax.random.fold_in(own_key, 2), number_of)[grade].astype(jnp.int32)


def centred(rng, extent, spread, limit, cuts=(), dtype=jnp.bfloat16):
    entries = jax.random.normal(rng, extent, jnp.float32) * spread
    if len(cuts) > 0:
        entries = block_levels(rng, extent, cuts, -0.22, 0.18) * entries
    return jnp.clip(entries, min=-limit, max=limit).astype(dtype)


def setup_inputs(seed: int = 0) -> dict:
    splits = jax.random.split(jax.random.key(seed), 7)
    return {
        "particles": centred(splits[0], (PARTS_SIZE, 3, NROWS, COLS), 1.0, 6.0, ((0, 16), (2, 8)), jnp.float32),
        "copies": place_ends(ranked(splits[1], (PARTS_SIZE,), PARTS_SIZE, 2), jax.random.fold_in(splits[1], 3), 0, PARTS_SIZE - 1).astype(jnp.int32),
        "depth_class": place_ends(jax.random.randint(splits[2], (NROWS, COLS), 0, CLASSES), jax.random.fold_in(splits[2], 1), 0, CLASSES - 1).astype(jnp.int32),
        "depth_table": jnp.clip(jnp.exp(jax.random.uniform(splits[3], (CLASSES,), jnp.float32, math.log(0.5), math.log(2.0))), 0.5, 2.0),
        "observed": centred(splits[4], (NROWS, COLS), 1.0, 6.0, ((0, 8),), jnp.float32),
        "nudge_gain": jnp.clip(jnp.exp(math.log(0.3) - 2.7080503 * jax.random.uniform(splits[5], (NROWS, COLS), jnp.float32) ** block_levels(splits[5], (NROWS, COLS), ((0, 8),), -0.2, 0.2)), 0.02, 0.3),
    }


time_step = 0.3
coriolis = 0.3


def depth_of(depth_class, depth_table):
    depth = jnp.zeros(depth_class.shape, jnp.float32)
    for klass in range(CLASSES):
        depth = jnp.where(depth_class == klass, depth_table[klass], depth)
    return depth


def col_diff(field):
    ahead = jnp.roll(field, -1, axis=-1)
    behind = jnp.roll(field, 1, axis=-1)
    ahead_two = jnp.roll(field, -2, axis=-1)
    behind_two = jnp.roll(field, 2, axis=-1)
    return (8.0 * (ahead - behind) - (ahead_two - behind_two)) / 12.0


def row_diff(padded):
    return (8.0 * (padded[..., 3:-1, :] - padded[..., 1:-3, :]) - (padded[..., 4:, :] - padded[..., :-4, :])) / 12.0


def pad_rows(field):
    return jnp.pad(field, ((2, 2), (0, 0)))


def reference(particles, copies, depth_class, depth_table, observed, nudge_gain):
    state = jnp.take(particles, copies.astype(jnp.int32), axis=0)
    depth = depth_of(depth_class, depth_table)

    def advance(single):
        height, east_vel, north_vel = single[0], single[1], single[2]
        for _ in range(STEPS):
            spread_div = col_diff(depth * east_vel) + row_diff(pad_rows(depth * north_vel))
            height = height - time_step * spread_div
            height = height + nudge_gain * (observed - height)
            new_east = east_vel + time_step * (-col_diff(height) + coriolis * north_vel)
            north_vel = north_vel + time_step * (-row_diff(pad_rows(height)) - coriolis * east_vel)
            east_vel = new_east
        return jnp.stack([height, east_vel, north_vel])

    return lax.map(advance, state)
```

```python
import functools

import jax
import jax.numpy as jnp
from jax import lax
from jax.experimental import pallas as pl
from jax.experimental.pallas import tpu as pltpu
from jax.sharding import PartitionSpec as P

MESH = pl.DeviceIdType.MESH
STEPS = 4
CLASSES = 8
ROWS = 64
PANELS = 8
PAD = 8
TILES = ROWS // 8
DT = 0.3
F0 = 0.3
K = DT / 12.0

PEERS = (
    (1, 0, 0), (0, 1, 0), (3, 0, 1), (2, 0, 0), (0, 1, 1),
    (1, 1, 0), (3, 1, 0), (2, 0, 1), (1, 0, 1), (3, 0, 0),
    (2, 1, 0), (1, 1, 1), (3, 1, 1), (2, 1, 1), (0, 0, 1),
)


def peer_of(me, step):
    x, z, c = me // 4, (me // 2) % 2, me % 2
    return ((x + step[0]) % 4) * 4 + ((z + step[1]) % 2) * 2 + (c + step[2]) % 2


def row_of(piece, d):
    tile = 2 + d // 4 if piece == 0 else d // 4 + 4 * (d // 8)
    return pl.multiple_of(tile * 8, 8)


def quarter_of(d):
    return d % 4


def kernel(
    copies, table, particles, classes, observed, gain, out,
    stage, cls, obs, gn, depth, state, flux, gathered0, gathered1, chosen, sent, got, g_halo,
    load_sem, halo_ss, halo_rs, g_ss, g_rs, ss1, rs1, ss2, rs2, self_sem,
):
    me, sp = lax.axis_index("dom"), lax.axis_index("space")
    gathered = (gathered0, gathered1)
    up, down = (sp + 7) % 8, (sp + 1) % 8

    loads = [
        pltpu.make_async_copy(classes, cls, load_sem.at[0]),
        pltpu.make_async_copy(particles, stage, load_sem.at[1]),
        pltpu.make_async_copy(gain, gn, load_sem.at[2]),
        pltpu.make_async_copy(observed, obs, load_sem.at[3]),
    ]
    for load in loads:
        load.start()

    barrier = pltpu.get_barrier_semaphore()
    for step in PEERS:
        pl.semaphore_signal(barrier, inc=1, device_id=(peer_of(me, step), sp), device_id_type=MESH)
    for other in (up, down):
        pl.semaphore_signal(barrier, inc=1, device_id=(me, other), device_id_type=MESH)

    lane = lax.broadcasted_iota(jnp.int32, (8, 128), 1)
    sublane = lax.broadcasted_iota(jnp.int32, (8, 128), 0)

    loads[0].wait()

    @pl.loop(0, TILES)
    def _(t):
        base = pl.multiple_of(t * 8, 8)
        for c in range(PANELS):
            kind = cls[pl.ds(base, 8), c * 128 : c * 128 + 128]
            d = jnp.zeros((8, 128), jnp.float32)
            for klass in range(CLASSES):
                d = jnp.where(kind == klass, table[klass], d)
            depth[c, pl.ds(base, 8), :] = d

    loads[1].wait()

    @pl.loop(0, 2 * TILES)
    def _(i):
        p, t = i // TILES, i % TILES
        base = pl.multiple_of(t * 8, 8)
        for c in range(PANELS):
            for f in range(3):
                v = stage[p, f, pl.ds(base, 8), c * 128 : c * 128 + 128]
                state[p, f, c, pl.ds(base + PAD, 8), :] = v
                if f == 2:
                    flux[p, c, pl.ds(base + PAD, 8), :] = depth[c, pl.ds(base, 8), :] * v

    loads[2].wait()
    loads[3].wait()

    def shifts(panels):
        ahead = [pltpu.roll(v, 127, 1) for v in panels]
        ahead2 = [pltpu.roll(v, 126, 1) for v in panels]
        behind = [pltpu.roll(v, 1, 1) for v in panels]
        behind2 = [pltpu.roll(v, 2, 1) for v in panels]
        found = []
        for c in range(PANELS):
            nxt, prv = (c + 1) % PANELS, (c - 1) % PANELS
            found.append((
                jnp.where(lane < 127, ahead[c], ahead[nxt]),
                jnp.where(lane >= 1, behind[c], behind[prv]),
                jnp.where(lane < 126, ahead2[c], ahead2[nxt]),
                jnp.where(lane >= 2, behind2[c], behind2[prv]),
            ))
        return found

    def height_of(p, base):
        panels = [
            depth[c, pl.ds(base, 8), :] * state[p, 1, c, pl.ds(base + PAD, 8), :]
            for c in range(PANELS)
        ]
        results = []
        for c, (a, b, a2, b2) in enumerate(shifts(panels)):
            ra = flux[p, c, pl.ds(base + PAD + 1, 8), :]
            rb = flux[p, c, pl.ds(base + PAD - 1, 8), :]
            ra2 = flux[p, c, pl.ds(base + PAD + 2, 8), :]
            rb2 = flux[p, c, pl.ds(base + PAD - 2, 8), :]
            div = 8.0 * ((a - b) + (ra - rb)) - ((a2 - b2) + (ra2 - rb2))
            h = state[p, 0, c, pl.ds(base + PAD, 8), :] - K * div
            g = gn[pl.ds(base, 8), c * 128 : c * 128 + 128]
            o = obs[pl.ds(base, 8), c * 128 : c * 128 + 128]
            results.append(h + g * (o - h))
        return results

    def height_tile(p, t, low, high):
        base = pl.multiple_of(t * 8, 8)
        inside = (base + sublane >= low) & (base + sublane < high)
        for c, h in enumerate(height_of(p, base)):
            old = state[p, 0, c, pl.ds(base + PAD, 8), :]
            state[p, 0, c, pl.ds(base + PAD, 8), :] = jnp.where(inside, h, old)

    def velocity_tile(p, t, low, high):
        base = pl.multiple_of(t * 8, 8)
        inside = (base + sublane >= low) & (base + sublane < high)
        panels = [state[p, 0, c, pl.ds(base + PAD, 8), :] for c in range(PANELS)]
        for c, (a, b, a2, b2) in enumerate(shifts(panels)):
            ra = state[p, 0, c, pl.ds(base + PAD + 1, 8), :]
            rb = state[p, 0, c, pl.ds(base + PAD - 1, 8), :]
            ra2 = state[p, 0, c, pl.ds(base + PAD + 2, 8), :]
            rb2 = state[p, 0, c, pl.ds(base + PAD - 2, 8), :]
            e = state[p, 1, c, pl.ds(base + PAD, 8), :]
            n = state[p, 2, c, pl.ds(base + PAD, 8), :]
            e_new = e - K * (8.0 * (a - b) - (a2 - b2)) + (DT * F0) * n
            n_new = n - K * (8.0 * (ra - rb) - (ra2 - rb2)) - (DT * F0) * e
            n_new = jnp.where(inside, n_new, n)
            state[p, 1, c, pl.ds(base + PAD, 8), :] = jnp.where(inside, e_new, e)
            state[p, 2, c, pl.ds(base + PAD, 8), :] = n_new
            flux[p, c, pl.ds(base + PAD, 8), :] = depth[c, pl.ds(base, 8), :] * n_new

    def halo_copies(k):
        return [
            pltpu.make_async_remote_copy(
                src_ref=sent.at[k, side],
                dst_ref=got.at[k, 1 - side],
                send_sem=halo_ss.at[k, side],
                recv_sem=halo_rs.at[k, 1 - side],
                device_id=(me, other),
                device_id_type=MESH,
            )
            for side, other in enumerate((up, down))
        ]

    def send_halo(k):
        @pl.loop(0, 2)
        def _(p):
            none = jnp.zeros((PANELS, 2, 128), jnp.float32)
            flux[p, :, PAD - 2 : PAD, :] = none
            flux[p, :, PAD + ROWS : PAD + ROWS + 2, :] = none
            for side, base, first in ((0, 0, 0), (1, ROWS - 8, 6)):
                for c, h in enumerate(height_of(p, base)):
                    f = flux[p, c, base + PAD : base + PAD + 8, :]
                    sent[k, side, c, pl.ds(p * 4, 2), :] = f[first : first + 2]
                    sent[k, side, c, pl.ds(p * 4 + 2, 2), :] = h[first : first + 2]

        for copy in halo_copies(k):
            copy.start()

    def take_halo(k):
        for copy in halo_copies(k):
            copy.wait_recv()
        top, bottom = sp > 0, sp < 7

        @pl.loop(0, 2)
        def _(p):
            for c in range(PANELS):
                first = flux[p, c, PAD : PAD + 1, :]
                second = flux[p, c, PAD + 1 : PAD + 2, :]
                last = flux[p, c, PAD + ROWS - 1 : PAD + ROWS, :]
                before = flux[p, c, PAD + ROWS - 2 : PAD + ROWS - 1, :]
                f_up = got[k, 0, c, pl.ds(p * 4, 2), :]
                f_down = got[k, 1, c, pl.ds(p * 4, 2), :]
                flux[p, c, PAD - 2 : PAD, :] = jnp.where(top, f_up, 0.0)
                flux[p, c, PAD + ROWS : PAD + ROWS + 2, :] = jnp.where(bottom, f_down, 0.0)
                cols = slice(c * 128, c * 128 + 128)
                for side, row, there, rest in (
                    (0, 0, PAD - 2, -first),
                    (0, 1, PAD - 1, 8.0 * first - second),
                    (1, 0, PAD + ROWS, before - 8.0 * last),
                    (1, 1, PAD + ROWS + 1, last),
                ):
                    near = row if side else row + 6
                    part = got[k, side, c, pl.ds(p * 4 + 2 + row, 1), :]
                    h = part - (1.0 - g_halo[side, near : near + 1, cols]) * (K * rest)
                    state[p, 0, c, there : there + 1, :] = jnp.where(bottom if side else top, h, 0.0)

    def inner(p):
        for k in range(1, STEPS + 1):

            @pl.loop((4 * k - 2) // 8, TILES - (4 * k - 2) // 8)
            def _(t):
                height_tile(p, t, 4 * k - 2, ROWS + 2 - 4 * k)

            @pl.loop(4 * k // 8, TILES - 4 * k // 8)
            def _(t):
                velocity_tile(p, t, 4 * k, ROWS - 4 * k)

    def outer(k):
        n = (4 * k - 2 + 7) // 8

        @pl.loop(0, 4 * n)
        def _(i):
            p, j = i // (2 * n), i % (2 * n)
            edge = j // n
            low = edge * (ROWS + 2 - 4 * k)
            height_tile(p, j + edge * (TILES - 2 * n), low, low + 4 * k - 2)

        m = (4 * k + 7) // 8

        @pl.loop(0, 4 * m)
        def _(i):
            p, j = i // (2 * m), i % (2 * m)
            edge = j // m
            low = edge * (ROWS - 4 * k)
            velocity_tile(p, j + edge * (TILES - 2 * m), low, low + 4 * k)

    def own_collect(piece):
        return pltpu.make_async_copy(
            state.at[:, :, pl.ds(2 * quarter_of(me), 2), pl.ds(PAD + row_of(piece, me), 8), :],
            gathered[piece].at[pl.ds(2 * me, 2)],
            self_sem.at[piece],
        )

    def collect(piece):
        for step in PEERS:
            d = peer_of(me, step)
            pltpu.make_async_remote_copy(
                src_ref=state.at[:, :, pl.ds(2 * quarter_of(d), 2), pl.ds(PAD + row_of(piece, d), 8), :],
                dst_ref=gathered[piece].at[pl.ds(2 * me, 2)],
                send_sem=ss1.at[piece],
                recv_sem=rs1.at[piece],
                device_id=(d, sp),
                device_id_type=MESH,
            ).start()
        own_collect(piece).start()

    def own_deliver(piece):
        return pltpu.make_async_copy(
            chosen.at[piece, pl.ds(2 * me, 2)],
            out.at[:, :, pl.ds(row_of(piece, me), 8), pl.ds(256 * quarter_of(me), 256)],
            self_sem.at[2 + piece],
        )

    def all_of(piece, sem):
        whole = gathered[piece].at[pl.ds(0, 30)]
        return pltpu.make_async_copy(whole, whole, sem.at[piece])

    def deliver(piece):
        all_of(piece, rs1).wait()
        own_collect(piece).wait()

        @pl.loop(0, 32)
        def _(j):
            source = copies[j]
            for f in range(3):
                for c in range(2):
                    chosen[piece, j, f, :, c * 128 : c * 128 + 128] = gathered[piece][source, f, c]

        for step in PEERS:
            d = peer_of(me, step)
            pltpu.make_async_remote_copy(
                src_ref=chosen.at[piece, pl.ds(2 * d, 2)],
                dst_ref=out.at[:, :, pl.ds(row_of(piece, me), 8), pl.ds(256 * quarter_of(me), 256)],
                send_sem=ss2.at[piece],
                recv_sem=rs2.at[piece],
                device_id=(d, sp),
                device_id_type=MESH,
            ).start()
        own_deliver(piece).start()

    g_copies = [
        pltpu.make_async_remote_copy(
            src_ref=gn.at[pl.ds(row, 8)],
            dst_ref=g_halo.at[1 - side, pl.ds(0, 8)],
            send_sem=g_ss.at[side],
            recv_sem=g_rs.at[1 - side],
            device_id=(me, other),
            device_id_type=MESH,
        )
        for side, other, row in ((0, up, 0), (1, down, ROWS - 8))
    ]

    pl.semaphore_wait(barrier, len(PEERS) + 2)
    send_halo(0)
    for copy in g_copies:
        copy.start()
    inner(0)
    inner(1)
    collect(0)
    for copy in g_copies:
        copy.wait_recv()
    for k in range(1, STEPS + 1):
        take_halo(k - 1)
        outer(k)
        if k < STEPS:
            send_halo(k)
    collect(1)
    deliver(0)
    deliver(1)
    for piece in range(2):
        all_of(piece, rs2).wait()
        own_deliver(piece).wait()
    for piece in range(2):
        all_of(piece, ss1).wait()
        all_of(piece, ss2).wait()
    for copy in g_copies:
        copy.wait_send()
    for k in range(STEPS):
        for copy in halo_copies(k):
            copy.wait_send()


def shards(particles, copies, depth_class, depth_table, observed, nudge_gain):
    f32 = jnp.float32
    sem = pltpu.SemaphoreType.DMA
    smem, anywhere = pl.BlockSpec(memory_space=pltpu.SMEM), pl.BlockSpec(memory_space=pl.ANY)
    return pl.pallas_call(
        kernel,
        out_shape=jax.ShapeDtypeStruct(particles.shape, f32),
        in_specs=[smem, smem, anywhere, anywhere, anywhere, anywhere],
        out_specs=anywhere,
        scratch_shapes=[
            pltpu.VMEM((2, 3, ROWS, 1024), f32),
            pltpu.VMEM((ROWS, 1024), jnp.int32),
            pltpu.VMEM((ROWS, 1024), f32),
            pltpu.VMEM((ROWS, 1024), f32),
            pltpu.VMEM((PANELS, ROWS, 128), f32),
            pltpu.VMEM((2, 3, PANELS, ROWS + 2 * PAD, 128), f32),
            pltpu.VMEM((2, PANELS, ROWS + 2 * PAD, 128), f32),
            pltpu.VMEM((32, 3, 2, 8, 128), f32),
            pltpu.VMEM((32, 3, 2, 8, 128), f32),
            pltpu.VMEM((2, 32, 3, 8, 256), f32),
            pltpu.VMEM((STEPS, 2, PANELS, 8, 128), f32),
            pltpu.VMEM((STEPS, 2, PANELS, 8, 128), f32),
            pltpu.VMEM((2, 8, 1024), f32),
            sem((4,)), sem((STEPS, 2)), sem((STEPS, 2)), sem((2,)), sem((2,)),
            sem((2,)), sem((2,)), sem((2,)), sem((2,)), sem((4,)),
        ],
        compiler_params=pltpu.CompilerParams(
            collective_id=0, has_side_effects=True, vmem_limit_bytes=40 * 2**20
        ),
    )(copies, depth_table, particles, depth_class, observed, nudge_gain)


def solution(mesh):
    placed = (
        P("dom", None, "space", None),
        P(),
        P("space", None),
        P(),
        P("space", None),
        P("space", None),
    )
    return jax.shard_map(
        shards, mesh=mesh, in_specs=placed, out_specs=P("dom", None, "space", None), check_vma=False
    )
```

```python
import functools

import jax
import jax.numpy as jnp
from jax import lax
from jax.experimental import pallas as pl
from jax.experimental.pallas import tpu as pltpu
from jax.sharding import PartitionSpec as P

MESH = pl.DeviceIdType.MESH
STEPS = 4
CLASSES = 8
ROWS = 64
PANELS = 8
PAD = 8
TILES = ROWS // 8
DT = 0.3
F0 = 0.3
K = DT / 12.0

PEERS = (
    (1, 0, 0), (0, 1, 0), (3, 0, 1), (2, 0, 0), (0, 1, 1),
    (1, 1, 0), (3, 1, 0), (2, 0, 1), (1, 0, 1), (3, 0, 0),
    (2, 1, 0), (1, 1, 1), (3, 1, 1), (2, 1, 1), (0, 0, 1),
)


def peer_of(me, step):
    x, z, c = me // 4, (me // 2) % 2, me % 2
    return ((x + step[0]) % 4) * 4 + ((z + step[1]) % 2) * 2 + (c + step[2]) % 2


def row_of(piece, d):
    tile = 2 + d // 4 if piece == 0 else d // 4 + 4 * (d // 8)
    return pl.multiple_of(tile * 8, 8)


def quarter_of(d):
    return d % 4


def kernel(
    copies_in, table_in, particles, classes, observed, gain, out,
    copies, table, stage, cls, obs, gn, depth, state, flux, gathered0, gathered1, chosen, sent, got, g_halo,
    load_sem, halo_ss, halo_rs, g_ss, g_rs, ss1, rs1, ss2, rs2, self_sem,
):
    me, sp = lax.axis_index("dom"), lax.axis_index("space")
    gathered = (gathered0, gathered1)
    up, down = (sp + 7) % 8, (sp + 1) % 8

    loads = [
        pltpu.make_async_copy(classes, cls, load_sem.at[0]),
        pltpu.make_async_copy(particles, stage, load_sem.at[1]),
        pltpu.make_async_copy(gain, gn, load_sem.at[2]),
        pltpu.make_async_copy(observed, obs, load_sem.at[3]),
        pltpu.make_async_copy(table_in, table, load_sem.at[4]),
        pltpu.make_async_copy(copies_in, copies, load_sem.at[5]),
    ]
    for load in loads:
        load.start()

    barrier = pltpu.get_barrier_semaphore()
    for step in PEERS:
        pl.semaphore_signal(barrier, inc=1, device_id=(peer_of(me, step), sp), device_id_type=MESH)
    for other in (up, down):
        pl.semaphore_signal(barrier, inc=1, device_id=(me, other), device_id_type=MESH)

    lane = lax.broadcasted_iota(jnp.int32, (8, 128), 1)
    sublane = lax.broadcasted_iota(jnp.int32, (8, 128), 0)

    loads[0].wait()
    loads[4].wait()

    @pl.loop(0, TILES)
    def _(t):
        base = pl.multiple_of(t * 8, 8)
        for c in range(PANELS):
            kind = cls[pl.ds(base, 8), c * 128 : c * 128 + 128]
            d = jnp.zeros((8, 128), jnp.float32)
            for klass in range(CLASSES):
                d = jnp.where(kind == klass, table[klass], d)
            depth[c, pl.ds(base, 8), :] = d

    loads[1].wait()

    @pl.loop(0, 2 * TILES)
    def _(i):
        p, t = i // TILES, i % TILES
        base = pl.multiple_of(t * 8, 8)
        for c in range(PANELS):
            for f in range(3):
                v = stage[p, f, pl.ds(base, 8), c * 128 : c * 128 + 128]
                state[p, f, c, pl.ds(base + PAD, 8), :] = v
                if f == 2:
                    flux[p, c, pl.ds(base + PAD, 8), :] = depth[c, pl.ds(base, 8), :] * v

    loads[2].wait()
    loads[3].wait()
    loads[5].wait()

    def shifts(panels):
        ahead = [pltpu.roll(v, 127, 1) for v in panels]
        ahead2 = [pltpu.roll(v, 126, 1) for v in panels]
        behind = [pltpu.roll(v, 1, 1) for v in panels]
        behind2 = [pltpu.roll(v, 2, 1) for v in panels]
        found = []
        for c in range(PANELS):
            nxt, prv = (c + 1) % PANELS, (c - 1) % PANELS
            found.append((
                jnp.where(lane < 127, ahead[c], ahead[nxt]),
                jnp.where(lane >= 1, behind[c], behind[prv]),
                jnp.where(lane < 126, ahead2[c], ahead2[nxt]),
                jnp.where(lane >= 2, behind2[c], behind2[prv]),
            ))
        return found

    def height_of(p, base):
        panels = [
            depth[c, pl.ds(base, 8), :] * state[p, 1, c, pl.ds(base + PAD, 8), :]
            for c in range(PANELS)
        ]
        results = []
        for c, (a, b, a2, b2) in enumerate(shifts(panels)):
            ra = flux[p, c, pl.ds(base + PAD + 1, 8), :]
            rb = flux[p, c, pl.ds(base + PAD - 1, 8), :]
            ra2 = flux[p, c, pl.ds(base + PAD + 2, 8), :]
            rb2 = flux[p, c, pl.ds(base + PAD - 2, 8), :]
            div = 8.0 * ((a - b) + (ra - rb)) - ((a2 - b2) + (ra2 - rb2))
            h = state[p, 0, c, pl.ds(base + PAD, 8), :] - K * div
            g = gn[pl.ds(base, 8), c * 128 : c * 128 + 128]
            o = obs[pl.ds(base, 8), c * 128 : c * 128 + 128]
            results.append(h + g * (o - h))
        return results

    def height_tile(t, low, high):
        base = pl.multiple_of(t * 8, 8)
        inside = (base + sublane >= low) & (base + sublane < high)
        found = [
            (p, c, jnp.where(inside, h, state[p, 0, c, pl.ds(base + PAD, 8), :]))
            for p in range(2)
            for c, h in enumerate(height_of(p, base))
        ]
        for p, c, h in found:
            state[p, 0, c, pl.ds(base + PAD, 8), :] = h

    def velocity_of(p, base, inside):
        panels = [state[p, 0, c, pl.ds(base + PAD, 8), :] for c in range(PANELS)]
        results = []
        for c, (a, b, a2, b2) in enumerate(shifts(panels)):
            ra = state[p, 0, c, pl.ds(base + PAD + 1, 8), :]
            rb = state[p, 0, c, pl.ds(base + PAD - 1, 8), :]
            ra2 = state[p, 0, c, pl.ds(base + PAD + 2, 8), :]
            rb2 = state[p, 0, c, pl.ds(base + PAD - 2, 8), :]
            e = state[p, 1, c, pl.ds(base + PAD, 8), :]
            n = state[p, 2, c, pl.ds(base + PAD, 8), :]
            e_new = e - K * (8.0 * (a - b) - (a2 - b2)) + (DT * F0) * n
            n_new = n - K * (8.0 * (ra - rb) - (ra2 - rb2)) - (DT * F0) * e
            n_new = jnp.where(inside, n_new, n)
            results.append((p, c, jnp.where(inside, e_new, e), n_new, depth[c, pl.ds(base, 8), :] * n_new))
        return results

    def velocity_tile(t, low, high):
        base = pl.multiple_of(t * 8, 8)
        inside = (base + sublane >= low) & (base + sublane < high)
        found = velocity_of(0, base, inside) + velocity_of(1, base, inside)
        for p, c, e, n, f in found:
            state[p, 1, c, pl.ds(base + PAD, 8), :] = e
            state[p, 2, c, pl.ds(base + PAD, 8), :] = n
            flux[p, c, pl.ds(base + PAD, 8), :] = f

    def halo_copies(k):
        return [
            pltpu.make_async_remote_copy(
                src_ref=sent.at[k, side],
                dst_ref=got.at[k, 1 - side],
                send_sem=halo_ss.at[k, side],
                recv_sem=halo_rs.at[k, 1 - side],
                device_id=(me, other),
                device_id_type=MESH,
            )
            for side, other in enumerate((up, down))
        ]

    def send_halo(k):
        none = jnp.zeros((PANELS, 2, 128), jnp.float32)
        for p in range(2):
            flux[p, :, PAD - 2 : PAD, :] = none
            flux[p, :, PAD + ROWS : PAD + ROWS + 2, :] = none
        found = [(p, side, height_of(p, side * (ROWS - 8))) for p in range(2) for side in range(2)]
        for p, side, heights in found:
            first, base = 6 * side, side * (ROWS - 8) + PAD
            for c, h in enumerate(heights):
                f = flux[p, c, base : base + 8, :]
                sent[k, side, c, p * 4 : p * 4 + 2, :] = f[first : first + 2]
                sent[k, side, c, p * 4 + 2 : p * 4 + 4, :] = h[first : first + 2]

        for copy in halo_copies(k):
            copy.start()

    def take_halo(k):
        for copy in halo_copies(k):
            copy.wait_recv()
        top, bottom = sp > 0, sp < 7

        @pl.loop(0, 2)
        def _(p):
            for c in range(PANELS):
                first = flux[p, c, PAD : PAD + 1, :]
                second = flux[p, c, PAD + 1 : PAD + 2, :]
                last = flux[p, c, PAD + ROWS - 1 : PAD + ROWS, :]
                before = flux[p, c, PAD + ROWS - 2 : PAD + ROWS - 1, :]
                f_up = got[k, 0, c, pl.ds(p * 4, 2), :]
                f_down = got[k, 1, c, pl.ds(p * 4, 2), :]
                flux[p, c, PAD - 2 : PAD, :] = jnp.where(top, f_up, 0.0)
                flux[p, c, PAD + ROWS : PAD + ROWS + 2, :] = jnp.where(bottom, f_down, 0.0)
                cols = slice(c * 128, c * 128 + 128)
                for side, row, there, rest in (
                    (0, 0, PAD - 2, -first),
                    (0, 1, PAD - 1, 8.0 * first - second),
                    (1, 0, PAD + ROWS, before - 8.0 * last),
                    (1, 1, PAD + ROWS + 1, last),
                ):
                    near = row if side else row + 6
                    part = got[k, side, c, pl.ds(p * 4 + 2 + row, 1), :]
                    h = part - (1.0 - g_halo[side, near : near + 1, cols]) * (K * rest)
                    state[p, 0, c, there : there + 1, :] = jnp.where(bottom if side else top, h, 0.0)

    def inner(*steps):
        for k in steps:

            @pl.loop((4 * k - 2) // 8, TILES - (4 * k - 2) // 8)
            def _(t):
                height_tile(t, 4 * k - 2, ROWS + 2 - 4 * k)

            @pl.loop(4 * k // 8, TILES - 4 * k // 8)
            def _(t):
                velocity_tile(t, 4 * k, ROWS - 4 * k)

    def outer(k):
        n = (4 * k - 2 + 7) // 8

        @pl.loop(0, 2 * n)
        def _(j):
            edge = j // n
            low = edge * (ROWS + 2 - 4 * k)
            height_tile(j + edge * (TILES - 2 * n), low, low + 4 * k - 2)

        def velocities(t, edge):
            low = edge * (ROWS - 4 * k)
            velocity_tile(t, low, low + 4 * k)

        @pl.loop(0, 2)
        def _(edge):
            velocities(edge * (TILES - 1), edge)

        if k < STEPS:
            send_halo(k)
        if k > 2:

            @pl.loop(0, 2)
            def _(edge):
                velocities(1 + edge * (TILES - 3), edge)

    def own_collect(piece):
        return pltpu.make_async_copy(
            state.at[:, :, pl.ds(2 * quarter_of(me), 2), pl.ds(PAD + row_of(piece, me), 8), :],
            gathered[piece].at[pl.ds(2 * me, 2)],
            self_sem.at[piece],
        )

    def collect(piece, first=0, last=len(PEERS)):
        for step in PEERS[first:last]:
            d = peer_of(me, step)
            pltpu.make_async_remote_copy(
                src_ref=state.at[:, :, pl.ds(2 * quarter_of(d), 2), pl.ds(PAD + row_of(piece, d), 8), :],
                dst_ref=gathered[piece].at[pl.ds(2 * me, 2)],
                send_sem=ss1.at[piece],
                recv_sem=rs1.at[piece],
                device_id=(d, sp),
                device_id_type=MESH,
            ).start()
        if last == len(PEERS):
            own_collect(piece).start()

    def own_deliver(piece):
        return pltpu.make_async_copy(
            chosen.at[piece, pl.ds(2 * me, 2)],
            out.at[:, :, pl.ds(row_of(piece, me), 8), pl.ds(256 * quarter_of(me), 256)],
            self_sem.at[2 + piece],
        )

    def all_of(piece, sem):
        whole = gathered[piece].at[pl.ds(0, 30)]
        return pltpu.make_async_copy(whole, whole, sem.at[piece])

    def deliver(piece):
        all_of(piece, rs1).wait()
        own_collect(piece).wait()

        @pl.loop(0, 32)
        def _(j):
            source = copies[j]
            for f in range(3):
                for c in range(2):
                    chosen[piece, j, f, :, c * 128 : c * 128 + 128] = gathered[piece][source, f, c]

        for step in PEERS:
            d = peer_of(me, step)
            pltpu.make_async_remote_copy(
                src_ref=chosen.at[piece, pl.ds(2 * d, 2)],
                dst_ref=out.at[:, :, pl.ds(row_of(piece, me), 8), pl.ds(256 * quarter_of(me), 256)],
                send_sem=ss2.at[piece],
                recv_sem=rs2.at[piece],
                device_id=(d, sp),
                device_id_type=MESH,
            ).start()
        own_deliver(piece).start()

    g_copies = [
        pltpu.make_async_remote_copy(
            src_ref=gn.at[pl.ds(row, 8)],
            dst_ref=g_halo.at[1 - side, pl.ds(0, 8)],
            send_sem=g_ss.at[side],
            recv_sem=g_rs.at[1 - side],
            device_id=(me, other),
            device_id_type=MESH,
        )
        for side, other, row in ((0, up, 0), (1, down, ROWS - 8))
    ]

    pl.semaphore_wait(barrier, len(PEERS) + 2)
    send_halo(0)
    for copy in g_copies:
        copy.start()
    inner(1)
    for copy in g_copies:
        copy.wait_recv()
    take_halo(0)
    outer(1)
    inner(2)
    take_halo(1)
    outer(2)
    inner(3)
    take_halo(2)
    outer(3)
    inner(4)
    collect(0)
    take_halo(3)
    outer(4)
    collect(1)
    deliver(0)
    deliver(1)
    for piece in range(2):
        all_of(piece, rs2).wait()
        own_deliver(piece).wait()
    for piece in range(2):
        all_of(piece, ss1).wait()
        all_of(piece, ss2).wait()
    for copy in g_copies:
        copy.wait_send()
    for k in range(STEPS):
        for copy in halo_copies(k):
            copy.wait_send()


def shards(particles, copies, depth_class, depth_table, observed, nudge_gain):
    f32 = jnp.float32
    sem = pltpu.SemaphoreType.DMA
    anywhere = pl.BlockSpec(memory_space=pl.ANY)
    return pl.pallas_call(
        kernel,
        out_shape=jax.ShapeDtypeStruct(particles.shape, f32),
        in_specs=[anywhere] * 6,
        out_specs=anywhere,
        scratch_shapes=[
            pltpu.SMEM((32,), jnp.int32),
            pltpu.SMEM((CLASSES,), f32),
            pltpu.VMEM((2, 3, ROWS, 1024), f32),
            pltpu.VMEM((ROWS, 1024), jnp.int32),
            pltpu.VMEM((ROWS, 1024), f32),
            pltpu.VMEM((ROWS, 1024), f32),
            pltpu.VMEM((PANELS, ROWS, 128), f32),
            pltpu.VMEM((2, 3, PANELS, ROWS + 2 * PAD, 128), f32),
            pltpu.VMEM((2, PANELS, ROWS + 2 * PAD, 128), f32),
            pltpu.VMEM((32, 3, 2, 8, 128), f32),
            pltpu.VMEM((32, 3, 2, 8, 128), f32),
            pltpu.VMEM((2, 32, 3, 8, 256), f32),
            pltpu.VMEM((STEPS, 2, PANELS, 8, 128), f32),
            pltpu.VMEM((STEPS, 2, PANELS, 8, 128), f32),
            pltpu.VMEM((2, 8, 1024), f32),
            sem((6,)), sem((STEPS, 2)), sem((STEPS, 2)), sem((2,)), sem((2,)),
            sem((2,)), sem((2,)), sem((2,)), sem((2,)), sem((4,)),
        ],
        compiler_params=pltpu.CompilerParams(
            collective_id=0, has_side_effects=True, vmem_limit_bytes=60 * 2**20
        ),
    )(copies, depth_table, particles, depth_class, observed, nudge_gain)


def solution(mesh):
    placed = (
        P("dom", None, "space", None),
        P(),
        P("space", None),
        P(),
        P("space", None),
        P("space", None),
    )
    return jax.shard_map(
        shards, mesh=mesh, in_specs=placed, out_specs=P("dom", None, "space", None), check_vma=False
    )
```

```python
import functools

import jax
import jax.numpy as jnp
from jax import lax
from jax.experimental import pallas as pl
from jax.experimental.pallas import tpu as pltpu
from jax.sharding import PartitionSpec as P

MESH = pl.DeviceIdType.MESH
STEPS = 4
CLASSES = 8
ROWS = 64
PANELS = 8
PAD = 16
TILES = ROWS // 8
DT = 0.3
F0 = 0.3
K = DT / 12.0

GROUP = 16


def peer_of(me, i):
    step = (i * 7) % GROUP
    x, z, c = me // 4 + step // 4, me // 2 + step // 2, me + step
    return (x % 4) * 4 + (z % 2) * 2 + c % 2


def row_of(piece, d):
    tile = 2 + d // 4 if piece == 0 else d // 4 + 4 * (d // 8)
    return pl.multiple_of(tile * 8, 8)


def quarter_of(d):
    return d % 4


def kernel(
    copies_in, table_in, particles, classes, observed, gain, out,
    copies, table, stage, cls, obs, gn, depth, keep, drive, state, flux, part, part_flux, gathered0, gathered1, chosen, sent, got,
    load_sem, halo_ss, halo_rs, fixed_ss, fixed_rs, ss1, rs1, ss2, rs2, self_sem,
):
    me, sp = lax.axis_index("dom"), lax.axis_index("space")
    gathered = (gathered0, gathered1)
    up, down = (sp + 7) % 8, (sp + 1) % 8

    loads = [
        pltpu.make_async_copy(classes, cls, load_sem.at[0]),
        pltpu.make_async_copy(particles, stage, load_sem.at[1]),
        pltpu.make_async_copy(gain, gn, load_sem.at[2]),
        pltpu.make_async_copy(observed, obs, load_sem.at[3]),
        pltpu.make_async_copy(table_in, table, load_sem.at[4]),
        pltpu.make_async_copy(copies_in, copies, load_sem.at[5]),
    ]
    for load in loads:
        load.start()

    barrier = pltpu.get_barrier_semaphore()

    @pl.loop(1, GROUP)
    def _(i):
        pl.semaphore_signal(barrier, inc=1, device_id=(peer_of(me, i), sp), device_id_type=MESH)

    for other in (up, down):
        pl.semaphore_signal(barrier, inc=1, device_id=(me, other), device_id_type=MESH)

    lane = lax.broadcasted_iota(jnp.int32, (8, 128), 1)
    sublane = lax.broadcasted_iota(jnp.int32, (8, 128), 0)

    loads[0].wait()
    loads[4].wait()

    @pl.loop(0, TILES)
    def _(t):
        base = pl.multiple_of(t * 8, 8)
        for c in range(PANELS):
            kind = cls[pl.ds(base, 8), c * 128 : c * 128 + 128]
            d = jnp.zeros((8, 128), jnp.float32)
            for klass in range(CLASSES):
                d = jnp.where(kind == klass, table[klass], d)
            depth[c, pl.ds(base + PAD, 8), :] = d

    loads[1].wait()

    @pl.loop(0, 2 * TILES)
    def _(i):
        p, t = i // TILES, i % TILES
        base = pl.multiple_of(t * 8, 8)
        for c in range(PANELS):
            for f in range(3):
                v = stage[p, f, pl.ds(base, 8), c * 128 : c * 128 + 128]
                state[p, f, c, pl.ds(base + PAD, 8), :] = v
                if f == 2:
                    flux[p, c, pl.ds(base + PAD, 8), :] = depth[c, pl.ds(base + PAD, 8), :] * v

    none = jnp.zeros((8, 128), jnp.float32)

    @pl.loop(0, 4)
    def _(i):
        row = pl.multiple_of((i % 2) * 8 + (i // 2) * (ROWS + PAD), 8)
        for c in range(PANELS):
            drive[c, pl.ds(row, 8), :] = none
            for p in range(2):
                flux[p, c, pl.ds(row, 8), :] = none
                for f in range(3):
                    state[p, f, c, pl.ds(row, 8), :] = none
        for side in range(2):
            for p in range(2):
                for c in range(PANELS):
                    part_flux[side, p, c, pl.ds(pl.multiple_of(i * 8, 8), 8), :] = none
                    for f in range(3):
                        part[side, p, f, c, pl.ds(pl.multiple_of(i * 8, 8), 8), :] = none

    loads[2].wait()
    loads[3].wait()
    loads[5].wait()

    @pl.loop(0, TILES)
    def _(t):
        base = pl.multiple_of(t * 8, 8)
        for c in range(PANELS):
            g = gn[pl.ds(base, 8), c * 128 : c * 128 + 128]
            keep[c, pl.ds(base + PAD, 8), :] = 1.0 - g
            drive[c, pl.ds(base + PAD, 8), :] = g * obs[pl.ds(base, 8), c * 128 : c * 128 + 128]

    def shifts(panels):
        ahead = [pltpu.roll(v, 127, 1) for v in panels]
        ahead2 = [pltpu.roll(v, 126, 1) for v in panels]
        behind = [pltpu.roll(v, 1, 1) for v in panels]
        behind2 = [pltpu.roll(v, 2, 1) for v in panels]
        found = []
        for c in range(PANELS):
            nxt, prv = (c + 1) % PANELS, (c - 1) % PANELS
            found.append((
                jnp.where(lane < 127, ahead[c], ahead[nxt]),
                jnp.where(lane >= 1, behind[c], behind[prv]),
                jnp.where(lane < 126, ahead2[c], ahead2[nxt]),
                jnp.where(lane >= 2, behind2[c], behind2[prv]),
            ))
        return found

    def columns_of(panels):
        return [8.0 * (a - b) - (a2 - b2) for a, b, a2, b2 in shifts(panels)]

    def heights_of(base, low, high):
        inside = (base + sublane >= low) & (base + sublane < high)
        here = pl.ds(base + PAD, 8)
        found = []
        for p in range(2):
            columns = columns_of([depth[c, here, :] * state[p, 1, c, here, :] for c in range(PANELS)])
            for c, along in enumerate(columns):
                a = flux[p, c, pl.ds(base + PAD + 1, 8), :]
                b = flux[p, c, pl.ds(base + PAD - 1, 8), :]
                a2 = flux[p, c, pl.ds(base + PAD + 2, 8), :]
                b2 = flux[p, c, pl.ds(base + PAD - 2, 8), :]
                old = state[p, 0, c, here, :]
                h = old - K * (along + (8.0 * (a - b) - (a2 - b2)))
                h = keep[c, here, :] * h + drive[c, here, :]
                found.append((p, c, jnp.where(inside, h, old)))
        return found

    def put_heights(base, low, high):
        for p, c, h in heights_of(base, low, high):
            state[p, 0, c, pl.ds(base + PAD, 8), :] = h

    def velocities_of(base):
        here = pl.ds(base + PAD, 8)
        found = []
        for p in range(2):
            for c, along in enumerate(columns_of([state[p, 0, c, here, :] for c in range(PANELS)])):
                a = state[p, 0, c, pl.ds(base + PAD + 1, 8), :]
                b = state[p, 0, c, pl.ds(base + PAD - 1, 8), :]
                a2 = state[p, 0, c, pl.ds(base + PAD + 2, 8), :]
                b2 = state[p, 0, c, pl.ds(base + PAD - 2, 8), :]
                e, n = state[p, 1, c, here, :], state[p, 2, c, here, :]
                e_new = e - K * along + (DT * F0) * n
                n_new = n - K * (8.0 * (a - b) - (a2 - b2)) - (DT * F0) * e
                found.append((p, c, e_new, n_new, depth[c, here, :] * n_new))
        return found

    def put_velocities(base):
        for p, c, e, n, f in velocities_of(base):
            state[p, 1, c, pl.ds(base + PAD, 8), :] = e
            state[p, 2, c, pl.ds(base + PAD, 8), :] = n
            flux[p, c, pl.ds(base + PAD, 8), :] = f

    def halo_copies(k):
        return [
            pltpu.make_async_remote_copy(
                src_ref=sent.at[k, side],
                dst_ref=got.at[k, 1 - side],
                send_sem=halo_ss.at[k, side],
                recv_sem=halo_rs.at[k, 1 - side],
                device_id=(me, other),
                device_id_type=MESH,
            )
            for side, other in enumerate((up, down))
        ]

    def send_halo(k):
        @pl.loop(0, 2)
        def _(side):
            base = pl.multiple_of(side * (ROWS - 8), 8)
            from_edge = sublane + side * (7 - 2 * sublane)
            for c in range(PANELS):
                f0, f1 = (flux[p, c, pl.ds(base + PAD, 8), :] for p in range(2))
                h0, h1 = (state[p, 0, c, pl.ds(base + PAD, 8), :] for p in range(2))
                second = jnp.where(side == 0, pltpu.roll(h0, 2, 0), pltpu.roll(h0, 6, 0))
                fourth = jnp.where(side == 0, pltpu.roll(h1, 6, 0), pltpu.roll(h1, 2, 0))
                sent[k, side, c, :, :] = jnp.where(
                    from_edge < 4,
                    jnp.where(from_edge < 2, f0, second),
                    jnp.where(from_edge < 6, pltpu.roll(f1, 4, 0), fourth),
                )

        for copy in halo_copies(k):
            copy.start()

    def inner(k):
        last = 8 - k

        @pl.loop(0, last + 1)
        def _(i):
            low = 4 * k - 2 + 8 * i
            put_heights(low - 4 * (i // last), low, ROWS + 2 - 4 * k)

        @pl.loop(0, 8 - k)
        def _(i):
            put_velocities(4 * k + 8 * i)

    def outer(k):
        @pl.loop(0, 2 * k)
        def _(j):
            edge, i = j % 2, j // 2
            put_heights(edge * ROWS - 4 * k + 8 * i, edge * (ROWS + 2 - 4 * k) - (1 - edge) * PAD, 4 * k - 2 + edge * (ROWS + PAD))

        send_halo(k - 1)

        @pl.loop(0, 2 * k)
        def _(j):
            edge, i = j % 2, j // 2
            put_velocities(edge * ROWS - 4 * k + 8 * i)

    def whole(k):
        @pl.loop(0, 13 - k)
        def _(i):
            put_heights(4 * k - 18 + 8 * i, -PAD, 82 - 4 * k)

        send_halo(k - 1)

        @pl.loop(0, 12 - k)
        def _(i):
            put_velocities(4 * k - 16 + 8 * i)

    def other_part(k):
        for copy in halo_copies(k - 1):
            copy.wait_recv()
        third = k // 3
        for side in range(2):
            there = sp < 7 if side else sp > 0
            near = slice(24, 32) if side else slice(0, 8)
            for c in range(PANELS):
                message = jnp.where(there, got[k - 1, side, c, :, :], 0.0)
                for p in range(2):
                    part_flux[side, p, c, near, :] = pltpu.roll(message, 4, 0) if p else message
                    part[side, p, 0, c, near, :] = pltpu.roll(message, 2 if side == p else 6, 0)

        @pl.loop(0, 2 + 2 * third)
        def _(j):
            side, i = j % 2, j // 2
            at = pl.multiple_of(8 + 8 * (side + i - 2 * side * i), 8)
            here = pl.ds(at, 8)
            own = pl.ds(pl.multiple_of(PAD - 8 + at + side * (ROWS - 16), 8), 8)
            found = []
            for p in range(2):
                columns = columns_of([depth[c, own, :] * part[side, p, 1, c, here, :] for c in range(PANELS)])
                for c, along in enumerate(columns):
                    a = part_flux[side, p, c, pl.ds(at + 1, 8), :]
                    b = part_flux[side, p, c, pl.ds(at - 1, 8), :]
                    a2 = part_flux[side, p, c, pl.ds(at + 2, 8), :]
                    b2 = part_flux[side, p, c, pl.ds(at - 2, 8), :]
                    h = part[side, p, 0, c, here, :] - K * (along + (8.0 * (a - b) - (a2 - b2)))
                    found.append((p, c, keep[c, own, :] * h))
            for p, c, h in found:
                part[side, p, 0, c, here, :] = h

        @pl.loop(0, 2 + 2 * third)
        def _(j):
            side, i = j % 2, j // 2
            at = pl.multiple_of(8 + 8 * (side + i - 2 * side * i), 8)
            here = pl.ds(at, 8)
            own = pl.ds(pl.multiple_of(PAD - 8 + at + side * (ROWS - 16), 8), 8)
            found = []
            for p in range(2):
                for c, along in enumerate(columns_of([part[side, p, 0, c, here, :] for c in range(PANELS)])):
                    a = part[side, p, 0, c, pl.ds(at + 1, 8), :]
                    b = part[side, p, 0, c, pl.ds(at - 1, 8), :]
                    a2 = part[side, p, 0, c, pl.ds(at + 2, 8), :]
                    b2 = part[side, p, 0, c, pl.ds(at - 2, 8), :]
                    e, n = part[side, p, 1, c, here, :], part[side, p, 2, c, here, :]
                    e_new = e - K * along + (DT * F0) * n
                    n_new = n - K * (8.0 * (a - b) - (a2 - b2)) - (DT * F0) * e
                    found.append((p, c, e_new, n_new, depth[c, own, :] * n_new))
            for p, c, e, n, f in found:
                part[side, p, 1, c, here, :] = e
                part[side, p, 2, c, here, :] = n
                part_flux[side, p, c, here, :] = f

    def join():
        @pl.loop(0, 4)
        def _(j):
            side, i = j % 2, j // 2
            here = pl.ds(pl.multiple_of(8 + 8 * i, 8), 8)
            own = pl.ds(pl.multiple_of(PAD + 8 * i + side * (ROWS - 16), 8), 8)
            found = [
                (p, f, c, state[p, f, c, own, :] + part[side, p, f, c, here, :])
                for p in range(2) for f in range(3) for c in range(PANELS)
            ]
            for p, f, c, v in found:
                state[p, f, c, own, :] = v

    def own_collect(piece):
        return pltpu.make_async_copy(
            state.at[:, :, pl.ds(2 * quarter_of(me), 2), pl.ds(PAD + row_of(piece, me), 8), :],
            gathered[piece].at[pl.ds(2 * me, 2)],
            self_sem.at[piece],
        )

    def collect(piece, first=1, last=GROUP):
        @pl.loop(first, last)
        def _(i):
            d = peer_of(me, i)
            pltpu.make_async_remote_copy(
                src_ref=state.at[:, :, pl.ds(2 * quarter_of(d), 2), pl.ds(PAD + row_of(piece, d), 8), :],
                dst_ref=gathered[piece].at[pl.ds(2 * me, 2)],
                send_sem=ss1.at[piece],
                recv_sem=rs1.at[piece],
                device_id=(d, sp),
                device_id_type=MESH,
            ).start()

        if last == GROUP:
            own_collect(piece).start()

    def own_deliver(piece):
        return pltpu.make_async_copy(
            chosen.at[piece, pl.ds(2 * me, 2)],
            out.at[:, :, pl.ds(row_of(piece, me), 8), pl.ds(256 * quarter_of(me), 256)],
            self_sem.at[2 + piece],
        )

    def all_of(piece, sem):
        whole = gathered[piece].at[pl.ds(0, 30)]
        return pltpu.make_async_copy(whole, whole, sem.at[piece])

    def deliver(piece):
        all_of(piece, rs1).wait()
        own_collect(piece).wait()

        @pl.loop(0, 32)
        def _(j):
            source = copies[j]
            for f in range(3):
                for c in range(2):
                    chosen[piece, j, f, :, c * 128 : c * 128 + 128] = gathered[piece][source, f, c]

        @pl.loop(1, GROUP)
        def _(i):
            d = peer_of(me, i)
            pltpu.make_async_remote_copy(
                src_ref=chosen.at[piece, pl.ds(2 * d, 2)],
                dst_ref=out.at[:, :, pl.ds(row_of(piece, me), 8), pl.ds(256 * quarter_of(me), 256)],
                send_sem=ss2.at[piece],
                recv_sem=rs2.at[piece],
                device_id=(d, sp),
                device_id_type=MESH,
            ).start()

        own_deliver(piece).start()

    fixed = [
        pltpu.make_async_remote_copy(
            src_ref=ref.at[:, pl.ds(source, 8), :],
            dst_ref=ref.at[:, pl.ds(target, 8), :],
            send_sem=fixed_ss.at[n, side],
            recv_sem=fixed_rs.at[n, 1 - side],
            device_id=(me, other),
            device_id_type=MESH,
        )
        for n, ref in enumerate((depth, keep))
        for side, other, source, target in ((0, up, PAD, PAD + ROWS), (1, down, PAD + ROWS - 8, PAD - 8))
    ]

    def take_fixed():
        for copy in fixed:
            copy.wait_recv()
        for there, row in ((sp > 0, PAD - 8), (sp < 7, PAD + ROWS)):
            for ref in (depth, keep):
                for c in range(PANELS):
                    ref[c, row : row + 8, :] = jnp.where(there, ref[c, row : row + 8, :], 0.0)

    pl.semaphore_wait(barrier, GROUP + 1)
    for copy in fixed:
        copy.start()
    inner(1)
    inner(2)
    take_fixed()

    @pl.loop(1, 3)
    def _(k):
        outer(k)


    @pl.loop(3, STEPS + 1)
    def _(k):
        whole(k)

    collect(0)

    @pl.loop(1, STEPS + 1)
    def _(k):
        other_part(k)

    join()
    collect(1)
    deliver(0)
    deliver(1)
    for piece in range(2):
        all_of(piece, rs2).wait()
        own_deliver(piece).wait()
    for piece in range(2):
        all_of(piece, ss1).wait()
        all_of(piece, ss2).wait()
    for copy in fixed:
        copy.wait_send()

    @pl.loop(0, STEPS)
    def _(k):
        for copy in halo_copies(k):
            copy.wait_send()


def shards(particles, copies, depth_class, depth_table, observed, nudge_gain):
    f32 = jnp.float32
    sem = pltpu.SemaphoreType.DMA
    anywhere = pl.BlockSpec(memory_space=pl.ANY)
    return pl.pallas_call(
        kernel,
        out_shape=jax.ShapeDtypeStruct(particles.shape, f32),
        in_specs=[anywhere] * 6,
        out_specs=anywhere,
        scratch_shapes=[
            pltpu.SMEM((32,), jnp.int32),
            pltpu.SMEM((CLASSES,), f32),
            pltpu.VMEM((2, 3, ROWS, 1024), f32),
            pltpu.VMEM((ROWS, 1024), jnp.int32),
            pltpu.VMEM((ROWS, 1024), f32),
            pltpu.VMEM((ROWS, 1024), f32),
            pltpu.VMEM((PANELS, ROWS + 2 * PAD, 128), f32),
            pltpu.VMEM((PANELS, ROWS + 2 * PAD, 128), f32),
            pltpu.VMEM((PANELS, ROWS + 2 * PAD, 128), f32),
            pltpu.VMEM((2, 3, PANELS, ROWS + 2 * PAD, 128), f32),
            pltpu.VMEM((2, PANELS, ROWS + 2 * PAD, 128), f32),
            pltpu.VMEM((2, 2, 3, PANELS, 32, 128), f32),
            pltpu.VMEM((2, 2, PANELS, 32, 128), f32),
            pltpu.VMEM((32, 3, 2, 8, 128), f32),
            pltpu.VMEM((32, 3, 2, 8, 128), f32),
            pltpu.VMEM((2, 32, 3, 8, 256), f32),
            pltpu.VMEM((STEPS, 2, PANELS, 8, 128), f32),
            pltpu.VMEM((STEPS, 2, PANELS, 8, 128), f32),
            sem((6,)), sem((STEPS, 2)), sem((STEPS, 2)), sem((2, 2)), sem((2, 2)),
            sem((2,)), sem((2,)), sem((2,)), sem((2,)), sem((4,)),
        ],
        compiler_params=pltpu.CompilerParams(
            collective_id=0, has_side_effects=True, vmem_limit_bytes=60 * 2**20
        ),
    )(copies, depth_table, particles, depth_class, observed, nudge_gain)


def solution(mesh):
    placed = (
        P("dom", None, "space", None),
        P(),
        P("space", None),
        P(),
        P("space", None),
        P("space", None),
    )
    return jax.shard_map(
        shards, mesh=mesh, in_specs=placed, out_specs=P("dom", None, "space", None), check_vma=False
    )
```

```python
import functools

import jax
import jax.numpy as jnp
from jax import lax
from jax.experimental import pallas as pl
from jax.experimental.pallas import tpu as pltpu
from jax.sharding import PartitionSpec as P

MESH = pl.DeviceIdType.MESH
STEPS = 4
CLASSES = 8
ROWS = 64
PANELS = 8
PAD = 16
TILES = ROWS // 8
DT = 0.3
F0 = 0.3
K = DT / 12.0

GROUP = 16


def peer_of(me, i):
    step = (i * 7) % GROUP
    x, z, c = me // 4 + step // 4, me // 2 + step // 2, me + step
    return (x % 4) * 4 + (z % 2) * 2 + c % 2


def row_of(piece, d):
    tile = 2 + d // 4 if piece == 0 else d // 4 + 4 * (d // 8)
    return pl.multiple_of(tile * 8, 8)


def quarter_of(d):
    return d % 4


def kernel(
    copies_in, table_in, particles, classes, observed, gain, out,
    copies, table, stage, cls, obs, gn, depth, keep, drive, state, flux, part, part_flux, band, gathered0, gathered1, chosen, sent, got,
    load_sem, halo_ss, halo_rs, fixed_ss, fixed_rs, ss1, rs1, ss2, rs2, self_sem,
):
    me, sp = lax.axis_index("dom"), lax.axis_index("space")
    gathered = (gathered0, gathered1)
    up, down = (sp + 7) % 8, (sp + 1) % 8

    loads = [
        pltpu.make_async_copy(classes, cls, load_sem.at[0]),
        pltpu.make_async_copy(particles, stage, load_sem.at[1]),
        pltpu.make_async_copy(gain, gn, load_sem.at[2]),
        pltpu.make_async_copy(observed, obs, load_sem.at[3]),
        pltpu.make_async_copy(table_in, table, load_sem.at[4]),
        pltpu.make_async_copy(copies_in, copies, load_sem.at[5]),
    ]
    for load in loads:
        load.start()

    barrier = pltpu.get_barrier_semaphore()

    @pl.loop(1, GROUP)
    def _(i):
        pl.semaphore_signal(barrier, inc=1, device_id=(peer_of(me, i), sp), device_id_type=MESH)

    for other in (up, down):
        pl.semaphore_signal(barrier, inc=1, device_id=(me, other), device_id_type=MESH)

    lane = lax.broadcasted_iota(jnp.int32, (8, 128), 1)
    sublane = lax.broadcasted_iota(jnp.int32, (8, 128), 0)

    row = lax.broadcasted_iota(jnp.int32, (512, 128), 0) % 256
    column = lax.broadcasted_iota(jnp.int32, (512, 128), 1)
    ahead = row - jnp.where(column < 64, column + 128, column)
    weights = jnp.where(ahead == 1, 8.0, 0.0) - jnp.where(ahead == -1, 8.0, 0.0)
    weights = weights - jnp.where(ahead == 2, 1.0, 0.0) + jnp.where(ahead == -2, 1.0, 0.0)
    band[...] = weights.astype(jnp.bfloat16)

    loads[0].wait()
    loads[4].wait()

    @pl.loop(0, TILES)
    def _(t):
        base = pl.multiple_of(t * 8, 8)
        for c in range(PANELS):
            kind = cls[pl.ds(base, 8), c * 128 : c * 128 + 128]
            d = jnp.zeros((8, 128), jnp.float32)
            for klass in range(CLASSES):
                d = jnp.where(kind == klass, table[klass], d)
            depth[c, pl.ds(base + PAD, 8), :] = d

    loads[1].wait()

    @pl.loop(0, 2 * TILES)
    def _(i):
        p, t = i // TILES, i % TILES
        base = pl.multiple_of(t * 8, 8)
        for c in range(PANELS):
            for f in range(3):
                v = stage[p, f, pl.ds(base, 8), c * 128 : c * 128 + 128]
                state[p, f, c, pl.ds(base + PAD, 8), :] = v
                if f == 2:
                    flux[p, c, pl.ds(base + PAD, 8), :] = depth[c, pl.ds(base + PAD, 8), :] * v

    none = jnp.zeros((8, 128), jnp.float32)

    @pl.loop(0, 4)
    def _(i):
        row = pl.multiple_of((i % 2) * 8 + (i // 2) * (ROWS + PAD), 8)
        for c in range(PANELS):
            drive[c, pl.ds(row, 8), :] = none
            for p in range(2):
                flux[p, c, pl.ds(row, 8), :] = none
                for f in range(3):
                    state[p, f, c, pl.ds(row, 8), :] = none
        for side in range(2):
            for p in range(2):
                for c in range(PANELS):
                    part_flux[side, p, c, pl.ds(pl.multiple_of(i * 8, 8), 8), :] = none
                    for f in range(3):
                        part[side, p, f, c, pl.ds(pl.multiple_of(i * 8, 8), 8), :] = none

    loads[2].wait()
    loads[3].wait()
    loads[5].wait()

    @pl.loop(0, TILES)
    def _(t):
        base = pl.multiple_of(t * 8, 8)
        for c in range(PANELS):
            g = gn[pl.ds(base, 8), c * 128 : c * 128 + 128]
            keep[c, pl.ds(base + PAD, 8), :] = 1.0 - g
            drive[c, pl.ds(base + PAD, 8), :] = g * obs[pl.ds(base, 8), c * 128 : c * 128 + 128]

    def shifts(panels):
        ahead = [pltpu.roll(v, 127, 1) for v in panels]
        ahead2 = [pltpu.roll(v, 126, 1) for v in panels]
        behind = [pltpu.roll(v, 1, 1) for v in panels]
        behind2 = [pltpu.roll(v, 2, 1) for v in panels]
        found = []
        for c in range(PANELS):
            nxt, prv = (c + 1) % PANELS, (c - 1) % PANELS
            found.append((
                jnp.where(lane < 127, ahead[c], ahead[nxt]),
                jnp.where(lane >= 1, behind[c], behind[prv]),
                jnp.where(lane < 126, ahead2[c], ahead2[nxt]),
                jnp.where(lane >= 2, behind2[c], behind2[prv]),
            ))
        return found

    def columns_of(panels):
        return [8.0 * (a - b) - (a2 - b2) for a, b, a2, b2 in shifts(panels)]

    def split_columns(panels):
        parts = []
        for c in range(PANELS):
            v = jnp.concatenate([panels[0][c], panels[1][c]], axis=0)
            high = v.astype(jnp.bfloat16)
            parts.append((high, (v - high.astype(jnp.float32)).astype(jnp.bfloat16)))
        rows = []
        for c in range(PANELS):
            here, ahead = parts[c], parts[(c + 1) % PANELS]
            rows.append(jnp.concatenate([here[0], ahead[0], here[1], ahead[1]], axis=1))
        product = jnp.dot(jnp.concatenate(rows, axis=0), band[...], preferred_element_type=jnp.float32)
        pieces = [product[16 * c : 16 * c + 16] for c in range(PANELS)]
        wide = lax.broadcasted_iota(jnp.int32, (16, 128), 1)
        found = [jnp.where(wide < 64, pieces[c - 1], pieces[c]) for c in range(PANELS)]
        return [v[:8] for v in found], [v[8:] for v in found]

    def all_columns(panels):
        if len(panels[0]) == 1:
            return [[columns_of(panels[p][0])] for p in range(2)]
        return [[columns_of(v) for v in panels[0]], split_columns(panels[1])]

    def put_heights(*windows):
        heres = [pl.ds(base + PAD, 8) for base, _, _ in windows]
        columns = all_columns(
            [[[depth[c, here, :] * state[p, 1, c, here, :] for c in range(PANELS)] for here in heres] for p in range(2)]
        )
        found = []
        for p in range(2):
            for w, (base, low, high) in enumerate(windows):
                inside = (base + sublane >= low) & (base + sublane < high)
                here = heres[w]
                for c, along in enumerate(columns[p][w]):
                    a = flux[p, c, pl.ds(base + PAD + 1, 8), :]
                    b = flux[p, c, pl.ds(base + PAD - 1, 8), :]
                    a2 = flux[p, c, pl.ds(base + PAD + 2, 8), :]
                    b2 = flux[p, c, pl.ds(base + PAD - 2, 8), :]
                    old = state[p, 0, c, here, :]
                    h = old - K * (along + (8.0 * (a - b) - (a2 - b2)))
                    h = keep[c, here, :] * h + drive[c, here, :]
                    found.append((p, c, here, jnp.where(inside, h, old)))
        for p, c, here, h in found:
            state[p, 0, c, here, :] = h

    def put_velocities(*bases):
        heres = [pl.ds(base + PAD, 8) for base in bases]
        columns = all_columns([[[state[p, 0, c, here, :] for c in range(PANELS)] for here in heres] for p in range(2)])
        found = []
        for p in range(2):
            for w, base in enumerate(bases):
                here = heres[w]
                for c, along in enumerate(columns[p][w]):
                    a = state[p, 0, c, pl.ds(base + PAD + 1, 8), :]
                    b = state[p, 0, c, pl.ds(base + PAD - 1, 8), :]
                    a2 = state[p, 0, c, pl.ds(base + PAD + 2, 8), :]
                    b2 = state[p, 0, c, pl.ds(base + PAD - 2, 8), :]
                    e, n = state[p, 1, c, here, :], state[p, 2, c, here, :]
                    e_new = e - K * along + (DT * F0) * n
                    n_new = n - K * (8.0 * (a - b) - (a2 - b2)) - (DT * F0) * e
                    found.append((p, c, here, e_new, n_new, depth[c, here, :] * n_new))
        for p, c, here, e, n, f in found:
            state[p, 1, c, here, :] = e
            state[p, 2, c, here, :] = n
            flux[p, c, here, :] = f

    def in_pairs(count, put, window):
        @pl.loop(0, count // 2)
        def _(i):
            put(window(i), window(i + count // 2))

        if count % 2:
            put(window(count - 1))

    def height_windows(count, window):
        in_pairs(count, put_heights, window)

    def velocity_windows(count, first):
        in_pairs(count, put_velocities, lambda i: first + 8 * i)

    def halo_copies(k):
        return [
            pltpu.make_async_remote_copy(
                src_ref=sent.at[k, side],
                dst_ref=got.at[k, 1 - side],
                send_sem=halo_ss.at[k, side],
                recv_sem=halo_rs.at[k, 1 - side],
                device_id=(me, other),
                device_id_type=MESH,
            )
            for side, other in enumerate((up, down))
        ]

    def send_halo(k):
        @pl.loop(0, 2)
        def _(side):
            base = pl.multiple_of(side * (ROWS - 8), 8)
            from_edge = sublane + side * (7 - 2 * sublane)
            for c in range(PANELS):
                f0, f1 = (flux[p, c, pl.ds(base + PAD, 8), :] for p in range(2))
                h0, h1 = (state[p, 0, c, pl.ds(base + PAD, 8), :] for p in range(2))
                second = jnp.where(side == 0, pltpu.roll(h0, 2, 0), pltpu.roll(h0, 6, 0))
                fourth = jnp.where(side == 0, pltpu.roll(h1, 6, 0), pltpu.roll(h1, 2, 0))
                sent[k, side, c, :, :] = jnp.where(
                    from_edge < 4,
                    jnp.where(from_edge < 2, f0, second),
                    jnp.where(from_edge < 6, pltpu.roll(f1, 4, 0), fourth),
                )

        for copy in halo_copies(k):
            copy.start()

    def inner(k):
        last = 8 - k

        def window(i):
            low = 4 * k - 2 + 8 * i
            return low - 4 * (i // last), low, ROWS + 2 - 4 * k

        height_windows(last + 1, window)
        velocity_windows(8 - k, 4 * k)

    def outer(k):
        @pl.loop(0, k)
        def _(i):
            put_heights(
                (8 * i - 4 * k, -PAD, 4 * k - 2), (ROWS - 4 * k + 8 * i, ROWS + 2 - 4 * k, ROWS + PAD)
            )

        send_halo(k - 1)

        @pl.loop(0, k)
        def _(i):
            put_velocities(8 * i - 4 * k, ROWS - 4 * k + 8 * i)

    def whole(k):
        height_windows(13 - k, lambda i: (4 * k - 18 + 8 * i, -PAD, 82 - 4 * k))
        send_halo(k - 1)
        velocity_windows(12 - k, 4 * k - 16)

    def other_part(k):
        for copy in halo_copies(k - 1):
            copy.wait_recv()
        third = k // 3
        for side in range(2):
            there = sp < 7 if side else sp > 0
            near = slice(24, 32) if side else slice(0, 8)
            for c in range(PANELS):
                message = jnp.where(there, got[k - 1, side, c, :, :], 0.0)
                for p in range(2):
                    part_flux[side, p, c, near, :] = pltpu.roll(message, 4, 0) if p else message
                    part[side, p, 0, c, near, :] = pltpu.roll(message, 2 if side == p else 6, 0)

        @pl.loop(0, 1 + third)
        def _(i):
            ats = (pl.multiple_of(8 + 8 * i, 8), pl.multiple_of(16 - 8 * i, 8))
            heres = [pl.ds(at, 8) for at in ats]
            owns = [pl.ds(pl.multiple_of(PAD - 8 + at + side * (ROWS - 16), 8), 8) for side, at in enumerate(ats)]
            columns = all_columns([
                [[depth[c, owns[side], :] * part[side, p, 1, c, heres[side], :] for c in range(PANELS)] for side in range(2)]
                for p in range(2)
            ])
            found = []
            for p in range(2):
                for side, at in enumerate(ats):
                    here, own = heres[side], owns[side]
                    for c, along in enumerate(columns[p][side]):
                        a = part_flux[side, p, c, pl.ds(at + 1, 8), :]
                        b = part_flux[side, p, c, pl.ds(at - 1, 8), :]
                        a2 = part_flux[side, p, c, pl.ds(at + 2, 8), :]
                        b2 = part_flux[side, p, c, pl.ds(at - 2, 8), :]
                        h = part[side, p, 0, c, here, :] - K * (along + (8.0 * (a - b) - (a2 - b2)))
                        found.append((side, p, c, here, keep[c, own, :] * h))
            for side, p, c, here, h in found:
                part[side, p, 0, c, here, :] = h

        @pl.loop(0, 1 + third)
        def _(i):
            ats = (pl.multiple_of(8 + 8 * i, 8), pl.multiple_of(16 - 8 * i, 8))
            heres = [pl.ds(at, 8) for at in ats]
            owns = [pl.ds(pl.multiple_of(PAD - 8 + at + side * (ROWS - 16), 8), 8) for side, at in enumerate(ats)]
            columns = all_columns([
                [[part[side, p, 0, c, heres[side], :] for c in range(PANELS)] for side in range(2)] for p in range(2)
            ])
            found = []
            for p in range(2):
                for side, at in enumerate(ats):
                    here, own = heres[side], owns[side]
                    for c, along in enumerate(columns[p][side]):
                        a = part[side, p, 0, c, pl.ds(at + 1, 8), :]
                        b = part[side, p, 0, c, pl.ds(at - 1, 8), :]
                        a2 = part[side, p, 0, c, pl.ds(at + 2, 8), :]
                        b2 = part[side, p, 0, c, pl.ds(at - 2, 8), :]
                        e, n = part[side, p, 1, c, here, :], part[side, p, 2, c, here, :]
                        e_new = e - K * along + (DT * F0) * n
                        n_new = n - K * (8.0 * (a - b) - (a2 - b2)) - (DT * F0) * e
                        found.append((side, p, c, here, e_new, n_new, depth[c, own, :] * n_new))
            for side, p, c, here, e, n, f in found:
                part[side, p, 1, c, here, :] = e
                part[side, p, 2, c, here, :] = n
                part_flux[side, p, c, here, :] = f

    def join():
        @pl.loop(0, 4)
        def _(j):
            side, i = j % 2, j // 2
            here = pl.ds(pl.multiple_of(8 + 8 * i, 8), 8)
            own = pl.ds(pl.multiple_of(PAD + 8 * i + side * (ROWS - 16), 8), 8)
            found = [
                (p, f, c, state[p, f, c, own, :] + part[side, p, f, c, here, :])
                for p in range(2) for f in range(3) for c in range(PANELS)
            ]
            for p, f, c, v in found:
                state[p, f, c, own, :] = v

    def own_collect(piece):
        return pltpu.make_async_copy(
            state.at[:, :, pl.ds(2 * quarter_of(me), 2), pl.ds(PAD + row_of(piece, me), 8), :],
            gathered[piece].at[pl.ds(2 * me, 2)],
            self_sem.at[piece],
        )

    def collect(piece, first=1, last=GROUP):
        @pl.loop(first, last)
        def _(i):
            d = peer_of(me, i)
            pltpu.make_async_remote_copy(
                src_ref=state.at[:, :, pl.ds(2 * quarter_of(d), 2), pl.ds(PAD + row_of(piece, d), 8), :],
                dst_ref=gathered[piece].at[pl.ds(2 * me, 2)],
                send_sem=ss1.at[piece],
                recv_sem=rs1.at[piece],
                device_id=(d, sp),
                device_id_type=MESH,
            ).start()

        if last == GROUP:
            own_collect(piece).start()

    def own_deliver(piece):
        return pltpu.make_async_copy(
            chosen.at[piece, pl.ds(2 * me, 2)],
            out.at[:, :, pl.ds(row_of(piece, me), 8), pl.ds(256 * quarter_of(me), 256)],
            self_sem.at[2 + piece],
        )

    def all_of(piece, sem):
        whole = gathered[piece].at[pl.ds(0, 30)]
        return pltpu.make_async_copy(whole, whole, sem.at[piece])

    def deliver(piece):
        all_of(piece, rs1).wait()
        own_collect(piece).wait()

        @pl.loop(0, 32)
        def _(j):
            source = copies[j]
            for f in range(3):
                for c in range(2):
                    chosen[piece, j, f, :, c * 128 : c * 128 + 128] = gathered[piece][source, f, c]

        @pl.loop(1, GROUP)
        def _(i):
            d = peer_of(me, i)
            pltpu.make_async_remote_copy(
                src_ref=chosen.at[piece, pl.ds(2 * d, 2)],
                dst_ref=out.at[:, :, pl.ds(row_of(piece, me), 8), pl.ds(256 * quarter_of(me), 256)],
                send_sem=ss2.at[piece],
                recv_sem=rs2.at[piece],
                device_id=(d, sp),
                device_id_type=MESH,
            ).start()

        own_deliver(piece).start()

    fixed = [
        pltpu.make_async_remote_copy(
            src_ref=ref.at[:, pl.ds(source, 8), :],
            dst_ref=ref.at[:, pl.ds(target, 8), :],
            send_sem=fixed_ss.at[n, side],
            recv_sem=fixed_rs.at[n, 1 - side],
            device_id=(me, other),
            device_id_type=MESH,
        )
        for n, ref in enumerate((depth, keep))
        for side, other, source, target in ((0, up, PAD, PAD + ROWS), (1, down, PAD + ROWS - 8, PAD - 8))
    ]

    def take_fixed():
        for copy in fixed:
            copy.wait_recv()
        for there, row in ((sp > 0, PAD - 8), (sp < 7, PAD + ROWS)):
            for ref in (depth, keep):
                for c in range(PANELS):
                    ref[c, row : row + 8, :] = jnp.where(there, ref[c, row : row + 8, :], 0.0)

    pl.semaphore_wait(barrier, GROUP + 1)
    for copy in fixed:
        copy.start()
    inner(1)
    inner(2)
    take_fixed()
    outer(1)
    outer(2)
    whole(3)
    whole(4)
    collect(0)

    @pl.loop(1, STEPS + 1)
    def _(k):
        other_part(k)

    join()
    collect(1)
    deliver(0)
    deliver(1)
    for piece in range(2):
        all_of(piece, rs2).wait()
        own_deliver(piece).wait()
    for piece in range(2):
        all_of(piece, ss1).wait()
        all_of(piece, ss2).wait()
    for copy in fixed:
        copy.wait_send()

    @pl.loop(0, STEPS)
    def _(k):
        for copy in halo_copies(k):
            copy.wait_send()


def shards(particles, copies, depth_class, depth_table, observed, nudge_gain):
    f32 = jnp.float32
    sem = pltpu.SemaphoreType.DMA
    anywhere = pl.BlockSpec(memory_space=pl.ANY)
    return pl.pallas_call(
        kernel,
        out_shape=jax.ShapeDtypeStruct(particles.shape, f32),
        in_specs=[anywhere] * 6,
        out_specs=anywhere,
        scratch_shapes=[
            pltpu.SMEM((32,), jnp.int32),
            pltpu.SMEM((CLASSES,), f32),
            pltpu.VMEM((2, 3, ROWS, 1024), f32),
            pltpu.VMEM((ROWS, 1024), jnp.int32),
            pltpu.VMEM((ROWS, 1024), f32),
            pltpu.VMEM((ROWS, 1024), f32),
            pltpu.VMEM((PANELS, ROWS + 2 * PAD, 128), f32),
            pltpu.VMEM((PANELS, ROWS + 2 * PAD, 128), f32),
            pltpu.VMEM((PANELS, ROWS + 2 * PAD, 128), f32),
            pltpu.VMEM((2, 3, PANELS, ROWS + 2 * PAD, 128), f32),
            pltpu.VMEM((2, PANELS, ROWS + 2 * PAD, 128), f32),
            pltpu.VMEM((2, 2, 3, PANELS, 32, 128), f32),
            pltpu.VMEM((2, 2, PANELS, 32, 128), f32),
            pltpu.VMEM((512, 128), jnp.bfloat16),
            pltpu.VMEM((32, 3, 2, 8, 128), f32),
            pltpu.VMEM((32, 3, 2, 8, 128), f32),
            pltpu.VMEM((2, 32, 3, 8, 256), f32),
            pltpu.VMEM((STEPS, 2, PANELS, 8, 128), f32),
            pltpu.VMEM((STEPS, 2, PANELS, 8, 128), f32),
            sem((6,)), sem((STEPS, 2)), sem((STEPS, 2)), sem((2, 2)), sem((2, 2)),
            sem((2,)), sem((2,)), sem((2,)), sem((2,)), sem((4,)),
        ],
        compiler_params=pltpu.CompilerParams(
            collective_id=0, has_side_effects=True, vmem_limit_bytes=60 * 2**20
        ),
    )(copies, depth_table, particles, depth_class, observed, nudge_gain)


def solution(mesh):
    placed = (
        P("dom", None, "space", None),
        P(),
        P("space", None),
        P(),
        P("space", None),
        P("space", None),
    )
    return jax.shard_map(
        shards, mesh=mesh, in_specs=placed, out_specs=P("dom", None, "space", None), check_vma=False
    )
```

```python
import functools

import jax
import jax.numpy as jnp
from jax import lax
from jax.experimental import pallas as pl
from jax.experimental.pallas import tpu as pltpu
from jax.sharding import PartitionSpec as P

MESH = pl.DeviceIdType.MESH
STEPS = 4
CLASSES = 8
ROWS = 64
PANELS = 8
PAD = 16
TILES = ROWS // 8
DT = 0.3
F0 = 0.3
K = DT / 12.0

GROUP = 16


def peer_of(me, i):
    step = (i * 7) % GROUP
    x, z, c = me // 4 + step // 4, me // 2 + step // 2, me + step
    return (x % 4) * 4 + (z % 2) * 2 + c % 2


def row_of(piece, d):
    tile = 2 + d // 4 if piece == 0 else d // 4 + 4 * (d // 8)
    return pl.multiple_of(tile * 8, 8)


def quarter_of(d):
    return d % 4


def kernel(
    copies_in, table_in, particles, classes, observed, gain, out,
    copies, table, stage, cls, obs, gn, depth, keep, drive, state, flux, part, part_flux, band, gathered0, gathered1, chosen, sent, got,
    load_sem, halo_ss, halo_rs, fixed_ss, fixed_rs, ss1, rs1, ss2, rs2, self_sem,
):
    me, sp = lax.axis_index("dom"), lax.axis_index("space")
    gathered = (gathered0, gathered1)
    up, down = (sp + 7) % 8, (sp + 1) % 8

    loads = [
        pltpu.make_async_copy(table_in, table, load_sem.at[0]),
        pltpu.make_async_copy(classes, cls, load_sem.at[1]),
        pltpu.make_async_copy(gain, gn, load_sem.at[2]),
        pltpu.make_async_copy(particles, stage, load_sem.at[3]),
        pltpu.make_async_copy(observed, obs, load_sem.at[4]),
        pltpu.make_async_copy(copies_in, copies, load_sem.at[5]),
    ]
    for load in loads:
        load.start()

    barrier = pltpu.get_barrier_semaphore()

    @pl.loop(1, GROUP)
    def _(i):
        pl.semaphore_signal(barrier, inc=1, device_id=(peer_of(me, i), sp), device_id_type=MESH)

    for other in (up, down):
        pl.semaphore_signal(barrier, inc=1, device_id=(me, other), device_id_type=MESH)

    lane = lax.broadcasted_iota(jnp.int32, (8, 128), 1)
    sublane = lax.broadcasted_iota(jnp.int32, (8, 128), 0)

    for load in loads[:3]:
        load.wait()

    @pl.loop(0, TILES)
    def _(t):
        base = pl.multiple_of(t * 8, 8)
        for c in range(PANELS):
            kind = cls[pl.ds(base, 8), c * 128 : c * 128 + 128]
            d = jnp.zeros((8, 128), jnp.float32)
            for klass in range(CLASSES):
                d = jnp.where(kind == klass, table[klass], d)
            depth[c, pl.ds(base + PAD, 8), :] = d
            keep[c, pl.ds(base + PAD, 8), :] = 1.0 - gn[pl.ds(base, 8), c * 128 : c * 128 + 128]

    def prepare():
        row = lax.broadcasted_iota(jnp.int32, (512, 128), 0) % 256
        column = lax.broadcasted_iota(jnp.int32, (512, 128), 1)
        ahead = row - jnp.where(column < 64, column + 128, column)
        weights = jnp.where(ahead == 1, 8.0, 0.0) - jnp.where(ahead == -1, 8.0, 0.0)
        weights = weights - jnp.where(ahead == 2, 1.0, 0.0) + jnp.where(ahead == -2, 1.0, 0.0)
        band[...] = weights.astype(jnp.bfloat16)

        for load in loads[3:]:
            load.wait()

        @pl.loop(0, 2 * TILES)
        def _(i):
            p, t = i // TILES, i % TILES
            base = pl.multiple_of(t * 8, 8)
            for c in range(PANELS):
                for f in range(3):
                    v = stage[p, f, pl.ds(base, 8), c * 128 : c * 128 + 128]
                    state[p, f, c, pl.ds(base + PAD, 8), :] = v
                    if f == 2:
                        flux[p, c, pl.ds(base + PAD, 8), :] = depth[c, pl.ds(base + PAD, 8), :] * v

        none = jnp.zeros((8, 128), jnp.float32)

        @pl.loop(0, 4)
        def _(i):
            row = pl.multiple_of((i % 2) * 8 + (i // 2) * (ROWS + PAD), 8)
            for c in range(PANELS):
                drive[c, pl.ds(row, 8), :] = none
                for p in range(2):
                    flux[p, c, pl.ds(row, 8), :] = none
                    for f in range(3):
                        state[p, f, c, pl.ds(row, 8), :] = none
            for side in range(2):
                for p in range(2):
                    for c in range(PANELS):
                        part_flux[side, p, c, pl.ds(pl.multiple_of(i * 8, 8), 8), :] = none
                        for f in range(3):
                            part[side, p, f, c, pl.ds(pl.multiple_of(i * 8, 8), 8), :] = none

        @pl.loop(0, TILES)
        def _(t):
            base = pl.multiple_of(t * 8, 8)
            for c in range(PANELS):
                cols = slice(c * 128, c * 128 + 128)
                drive[c, pl.ds(base + PAD, 8), :] = gn[pl.ds(base, 8), cols] * obs[pl.ds(base, 8), cols]

    def shifts(panels):
        ahead = [pltpu.roll(v, 127, 1) for v in panels]
        ahead2 = [pltpu.roll(v, 126, 1) for v in panels]
        behind = [pltpu.roll(v, 1, 1) for v in panels]
        behind2 = [pltpu.roll(v, 2, 1) for v in panels]
        found = []
        for c in range(PANELS):
            nxt, prv = (c + 1) % PANELS, (c - 1) % PANELS
            found.append((
                jnp.where(lane < 127, ahead[c], ahead[nxt]),
                jnp.where(lane >= 1, behind[c], behind[prv]),
                jnp.where(lane < 126, ahead2[c], ahead2[nxt]),
                jnp.where(lane >= 2, behind2[c], behind2[prv]),
            ))
        return found

    def columns_of(panels):
        return [8.0 * (a - b) - (a2 - b2) for a, b, a2, b2 in shifts(panels)]

    def split_columns(panels):
        parts = []
        for c in range(PANELS):
            v = jnp.concatenate([panels[0][c], panels[1][c]], axis=0)
            high = v.astype(jnp.bfloat16)
            parts.append((high, (v - high.astype(jnp.float32)).astype(jnp.bfloat16)))
        rows = []
        for c in range(PANELS):
            here, ahead = parts[c], parts[(c + 1) % PANELS]
            rows.append(jnp.concatenate([here[0], ahead[0], here[1], ahead[1]], axis=1))
        product = jnp.dot(jnp.concatenate(rows, axis=0), band[...], preferred_element_type=jnp.float32)
        pieces = [product[16 * c : 16 * c + 16] for c in range(PANELS)]
        wide = lax.broadcasted_iota(jnp.int32, (16, 128), 1)
        found = [jnp.where(wide < 64, pieces[c - 1], pieces[c]) for c in range(PANELS)]
        return [v[:8] for v in found], [v[8:] for v in found]

    def all_columns(panels):
        if len(panels[0]) == 1:
            return [[columns_of(panels[p][0])] for p in range(2)]
        return [[columns_of(v) for v in panels[0]], split_columns(panels[1])]

    def put_heights(*windows):
        heres = [pl.ds(base + PAD, 8) for base, _, _ in windows]
        columns = all_columns(
            [[[depth[c, here, :] * state[p, 1, c, here, :] for c in range(PANELS)] for here in heres] for p in range(2)]
        )
        found = []
        for p in range(2):
            for w, (base, low, high) in enumerate(windows):
                inside = (base + sublane >= low) & (base + sublane < high)
                here = heres[w]
                for c, along in enumerate(columns[p][w]):
                    a = flux[p, c, pl.ds(base + PAD + 1, 8), :]
                    b = flux[p, c, pl.ds(base + PAD - 1, 8), :]
                    a2 = flux[p, c, pl.ds(base + PAD + 2, 8), :]
                    b2 = flux[p, c, pl.ds(base + PAD - 2, 8), :]
                    old = state[p, 0, c, here, :]
                    h = old - K * (along + (8.0 * (a - b) - (a2 - b2)))
                    h = keep[c, here, :] * h + drive[c, here, :]
                    found.append((p, c, here, jnp.where(inside, h, old)))
        for p, c, here, h in found:
            state[p, 0, c, here, :] = h

    def put_velocities(*bases):
        heres = [pl.ds(base + PAD, 8) for base in bases]
        columns = all_columns([[[state[p, 0, c, here, :] for c in range(PANELS)] for here in heres] for p in range(2)])
        found = []
        for p in range(2):
            for w, base in enumerate(bases):
                here = heres[w]
                for c, along in enumerate(columns[p][w]):
                    a = state[p, 0, c, pl.ds(base + PAD + 1, 8), :]
                    b = state[p, 0, c, pl.ds(base + PAD - 1, 8), :]
                    a2 = state[p, 0, c, pl.ds(base + PAD + 2, 8), :]
                    b2 = state[p, 0, c, pl.ds(base + PAD - 2, 8), :]
                    e, n = state[p, 1, c, here, :], state[p, 2, c, here, :]
                    e_new = e - K * along + (DT * F0) * n
                    n_new = n - K * (8.0 * (a - b) - (a2 - b2)) - (DT * F0) * e
                    found.append((p, c, here, e_new, n_new, depth[c, here, :] * n_new))
        for p, c, here, e, n, f in found:
            state[p, 1, c, here, :] = e
            state[p, 2, c, here, :] = n
            flux[p, c, here, :] = f

    def in_pairs(count, put, window):
        @pl.loop(0, count // 2)
        def _(i):
            put(window(i), window(i + count // 2))

        if count % 2:
            put(window(count - 1))

    def height_windows(count, window):
        in_pairs(count, put_heights, window)

    def velocity_windows(count, first):
        in_pairs(count, put_velocities, lambda i: first + 8 * i)

    def halo_copies(k):
        return [
            pltpu.make_async_remote_copy(
                src_ref=sent.at[k, side],
                dst_ref=got.at[k, 1 - side],
                send_sem=halo_ss.at[k, side],
                recv_sem=halo_rs.at[k, 1 - side],
                device_id=(me, other),
                device_id_type=MESH,
            )
            for side, other in enumerate((up, down))
        ]

    def send_halo(k):
        @pl.loop(0, 2)
        def _(side):
            base = pl.multiple_of(side * (ROWS - 8), 8)
            from_edge = sublane + side * (7 - 2 * sublane)
            for c in range(PANELS):
                f0, f1 = (flux[p, c, pl.ds(base + PAD, 8), :] for p in range(2))
                h0, h1 = (state[p, 0, c, pl.ds(base + PAD, 8), :] for p in range(2))
                second = jnp.where(side == 0, pltpu.roll(h0, 2, 0), pltpu.roll(h0, 6, 0))
                fourth = jnp.where(side == 0, pltpu.roll(h1, 6, 0), pltpu.roll(h1, 2, 0))
                sent[k, side, c, :, :] = jnp.where(
                    from_edge < 4,
                    jnp.where(from_edge < 2, f0, second),
                    jnp.where(from_edge < 6, pltpu.roll(f1, 4, 0), fourth),
                )

        for copy in halo_copies(k):
            copy.start()

    def inner(k):
        last = 8 - k

        def window(i):
            low = 4 * k - 2 + 8 * i
            return low - 4 * (i // last), low, ROWS + 2 - 4 * k

        height_windows(last + 1, window)
        velocity_windows(8 - k, 4 * k)

    def outer(k):
        @pl.loop(0, k)
        def _(i):
            put_heights(
                (8 * i - 4 * k, -PAD, 4 * k - 2), (ROWS - 4 * k + 8 * i, ROWS + 2 - 4 * k, ROWS + PAD)
            )

        send_halo(k - 1)

        @pl.loop(0, k)
        def _(i):
            put_velocities(8 * i - 4 * k, ROWS - 4 * k + 8 * i)

    def whole(k):
        height_windows(13 - k, lambda i: (4 * k - 18 + 8 * i, -PAD, 82 - 4 * k))
        send_halo(k - 1)
        velocity_windows(12 - k, 4 * k - 16)

    def other_part(k):
        for copy in halo_copies(k - 1):
            copy.wait_recv()
        third = k // 3
        for side in range(2):
            there = sp < 7 if side else sp > 0
            near = slice(24, 32) if side else slice(0, 8)
            for c in range(PANELS):
                message = jnp.where(there, got[k - 1, side, c, :, :], 0.0)
                for p in range(2):
                    part_flux[side, p, c, near, :] = pltpu.roll(message, 4, 0) if p else message
                    part[side, p, 0, c, near, :] = pltpu.roll(message, 2 if side == p else 6, 0)

        @pl.loop(0, 1 + third)
        def _(i):
            ats = (pl.multiple_of(8 + 8 * i, 8), pl.multiple_of(16 - 8 * i, 8))
            heres = [pl.ds(at, 8) for at in ats]
            owns = [pl.ds(pl.multiple_of(PAD - 8 + at + side * (ROWS - 16), 8), 8) for side, at in enumerate(ats)]
            columns = all_columns([
                [[depth[c, owns[side], :] * part[side, p, 1, c, heres[side], :] for c in range(PANELS)] for side in range(2)]
                for p in range(2)
            ])
            found = []
            for p in range(2):
                for side, at in enumerate(ats):
                    here, own = heres[side], owns[side]
                    for c, along in enumerate(columns[p][side]):
                        a = part_flux[side, p, c, pl.ds(at + 1, 8), :]
                        b = part_flux[side, p, c, pl.ds(at - 1, 8), :]
                        a2 = part_flux[side, p, c, pl.ds(at + 2, 8), :]
                        b2 = part_flux[side, p, c, pl.ds(at - 2, 8), :]
                        h = part[side, p, 0, c, here, :] - K * (along + (8.0 * (a - b) - (a2 - b2)))
                        found.append((side, p, c, here, keep[c, own, :] * h))
            for side, p, c, here, h in found:
                part[side, p, 0, c, here, :] = h

        @pl.loop(0, 1 + third)
        def _(i):
            ats = (pl.multiple_of(8 + 8 * i, 8), pl.multiple_of(16 - 8 * i, 8))
            heres = [pl.ds(at, 8) for at in ats]
            owns = [pl.ds(pl.multiple_of(PAD - 8 + at + side * (ROWS - 16), 8), 8) for side, at in enumerate(ats)]
            columns = all_columns([
                [[part[side, p, 0, c, heres[side], :] for c in range(PANELS)] for side in range(2)] for p in range(2)
            ])
            found = []
            for p in range(2):
                for side, at in enumerate(ats):
                    here, own = heres[side], owns[side]
                    for c, along in enumerate(columns[p][side]):
                        a = part[side, p, 0, c, pl.ds(at + 1, 8), :]
                        b = part[side, p, 0, c, pl.ds(at - 1, 8), :]
                        a2 = part[side, p, 0, c, pl.ds(at + 2, 8), :]
                        b2 = part[side, p, 0, c, pl.ds(at - 2, 8), :]
                        e, n = part[side, p, 1, c, here, :], part[side, p, 2, c, here, :]
                        e_new = e - K * along + (DT * F0) * n
                        n_new = n - K * (8.0 * (a - b) - (a2 - b2)) - (DT * F0) * e
                        found.append((side, p, c, here, e_new, n_new, depth[c, own, :] * n_new))
            for side, p, c, here, e, n, f in found:
                part[side, p, 1, c, here, :] = e
                part[side, p, 2, c, here, :] = n
                part_flux[side, p, c, here, :] = f

    def join():
        @pl.loop(0, 4)
        def _(j):
            side, i = j % 2, j // 2
            here = pl.ds(pl.multiple_of(8 + 8 * i, 8), 8)
            own = pl.ds(pl.multiple_of(PAD + 8 * i + side * (ROWS - 16), 8), 8)
            found = [
                (p, f, c, state[p, f, c, own, :] + part[side, p, f, c, here, :])
                for p in range(2) for f in range(3) for c in range(PANELS)
            ]
            for p, f, c, v in found:
                state[p, f, c, own, :] = v

    def own_collect(piece):
        return pltpu.make_async_copy(
            state.at[:, :, pl.ds(2 * quarter_of(me), 2), pl.ds(PAD + row_of(piece, me), 8), :],
            gathered[piece].at[pl.ds(2 * me, 2)],
            self_sem.at[piece],
        )

    def collect(piece, first=1, last=GROUP):
        @pl.loop(first, last)
        def _(i):
            d = peer_of(me, i)
            pltpu.make_async_remote_copy(
                src_ref=state.at[:, :, pl.ds(2 * quarter_of(d), 2), pl.ds(PAD + row_of(piece, d), 8), :],
                dst_ref=gathered[piece].at[pl.ds(2 * me, 2)],
                send_sem=ss1.at[piece],
                recv_sem=rs1.at[piece],
                device_id=(d, sp),
                device_id_type=MESH,
            ).start()

        if last == GROUP:
            own_collect(piece).start()

    def own_deliver(piece):
        return pltpu.make_async_copy(
            chosen.at[piece, pl.ds(2 * me, 2)],
            out.at[:, :, pl.ds(row_of(piece, me), 8), pl.ds(256 * quarter_of(me), 256)],
            self_sem.at[2 + piece],
        )

    def all_of(piece, sem):
        whole = gathered[piece].at[pl.ds(0, 30)]
        return pltpu.make_async_copy(whole, whole, sem.at[piece])

    def deliver(piece):
        all_of(piece, rs1).wait()
        own_collect(piece).wait()

        def pick(d):
            sources = [copies[2 * d + slot] for slot in range(2)]
            picked = [gathered[piece][source, f, c] for source in sources for f in range(3) for c in range(2)]
            for n, v in enumerate(picked):
                f, c = n // 2 % 3, n % 2
                chosen[piece, 2 * d + n // 6, f, :, c * 128 : c * 128 + 128] = v

        @pl.loop(1, GROUP)
        def _(i):
            d = peer_of(me, i)
            pick(d)
            pltpu.make_async_remote_copy(
                src_ref=chosen.at[piece, pl.ds(2 * d, 2)],
                dst_ref=out.at[:, :, pl.ds(row_of(piece, me), 8), pl.ds(256 * quarter_of(me), 256)],
                send_sem=ss2.at[piece],
                recv_sem=rs2.at[piece],
                device_id=(d, sp),
                device_id_type=MESH,
            ).start()

        pick(me)
        own_deliver(piece).start()

    fixed = [
        pltpu.make_async_remote_copy(
            src_ref=ref.at[:, pl.ds(source, 8), :],
            dst_ref=ref.at[:, pl.ds(target, 8), :],
            send_sem=fixed_ss.at[n, side],
            recv_sem=fixed_rs.at[n, 1 - side],
            device_id=(me, other),
            device_id_type=MESH,
        )
        for n, ref in enumerate((depth, keep))
        for side, other, source, target in ((0, up, PAD, PAD + ROWS), (1, down, PAD + ROWS - 8, PAD - 8))
    ]

    def take_fixed():
        for copy in fixed:
            copy.wait_recv()
        for there, row in ((sp > 0, PAD - 8), (sp < 7, PAD + ROWS)):
            for ref in (depth, keep):
                for c in range(PANELS):
                    ref[c, row : row + 8, :] = jnp.where(there, ref[c, row : row + 8, :], 0.0)

    pl.semaphore_wait(barrier, GROUP + 1)
    for copy in fixed:
        copy.start()
    prepare()
    inner(1)
    inner(2)
    take_fixed()
    outer(1)
    outer(2)
    whole(3)
    whole(4)
    collect(0)

    @pl.loop(1, STEPS + 1)
    def _(k):
        other_part(k)

    join()
    collect(1)
    deliver(0)
    deliver(1)
    for piece in range(2):
        all_of(piece, rs2).wait()
        own_deliver(piece).wait()
    for piece in range(2):
        all_of(piece, ss1).wait()
        all_of(piece, ss2).wait()
    for copy in fixed:
        copy.wait_send()

    @pl.loop(0, STEPS)
    def _(k):
        for copy in halo_copies(k):
            copy.wait_send()


def shards(particles, copies, depth_class, depth_table, observed, nudge_gain):
    f32 = jnp.float32
    sem = pltpu.SemaphoreType.DMA
    anywhere = pl.BlockSpec(memory_space=pl.ANY)
    return pl.pallas_call(
        kernel,
        out_shape=jax.ShapeDtypeStruct(particles.shape, f32),
        in_specs=[anywhere] * 6,
        out_specs=anywhere,
        scratch_shapes=[
            pltpu.SMEM((32,), jnp.int32),
            pltpu.SMEM((CLASSES,), f32),
            pltpu.VMEM((2, 3, ROWS, 1024), f32),
            pltpu.VMEM((ROWS, 1024), jnp.int32),
            pltpu.VMEM((ROWS, 1024), f32),
            pltpu.VMEM((ROWS, 1024), f32),
            pltpu.VMEM((PANELS, ROWS + 2 * PAD, 128), f32),
            pltpu.VMEM((PANELS, ROWS + 2 * PAD, 128), f32),
            pltpu.VMEM((PANELS, ROWS + 2 * PAD, 128), f32),
            pltpu.VMEM((2, 3, PANELS, ROWS + 2 * PAD, 128), f32),
            pltpu.VMEM((2, PANELS, ROWS + 2 * PAD, 128), f32),
            pltpu.VMEM((2, 2, 3, PANELS, 32, 128), f32),
            pltpu.VMEM((2, 2, PANELS, 32, 128), f32),
            pltpu.VMEM((512, 128), jnp.bfloat16),
            pltpu.VMEM((32, 3, 2, 8, 128), f32),
            pltpu.VMEM((32, 3, 2, 8, 128), f32),
            pltpu.VMEM((2, 32, 3, 8, 256), f32),
            pltpu.VMEM((STEPS, 2, PANELS, 8, 128), f32),
            pltpu.VMEM((STEPS, 2, PANELS, 8, 128), f32),
            sem((6,)), sem((STEPS, 2)), sem((STEPS, 2)), sem((2, 2)), sem((2, 2)),
            sem((2,)), sem((2,)), sem((2,)), sem((2,)), sem((4,)),
        ],
        compiler_params=pltpu.CompilerParams(
            collective_id=0, has_side_effects=True, vmem_limit_bytes=60 * 2**20
        ),
    )(copies, depth_table, particles, depth_class, observed, nudge_gain)


def solution(mesh):
    placed = (
        P("dom", None, "space", None),
        P(),
        P("space", None),
        P(),
        P("space", None),
        P("space", None),
    )
    return jax.shard_map(
        shards, mesh=mesh, in_specs=placed, out_specs=P("dom", None, "space", None), check_vma=False
    )
```

```python
import functools

import jax
import jax.numpy as jnp
from jax import lax
from jax.experimental import pallas as pl
from jax.experimental.pallas import tpu as pltpu
from jax.sharding import PartitionSpec as P

MESH = pl.DeviceIdType.MESH
STEPS = 4
CLASSES = 8
ROWS = 64
PANELS = 8
PAD = 16
TILES = ROWS // 8
DT = 0.3
F0 = 0.3
K = DT / 12.0

GROUP = 16


def peer_of(me, i):
    step = (i * 7) % GROUP
    x, z, c = me // 4 + step // 4, me // 2 + step // 2, me + step
    return (x % 4) * 4 + (z % 2) * 2 + c % 2


def row_of(piece, d):
    tile = 2 + d // 4 if piece == 0 else d // 4 + 4 * (d // 8)
    return pl.multiple_of(tile * 8, 8)


def quarter_of(d):
    return d % 4


def kernel(
    copies_in, table_in, particles, classes, observed, gain, out,
    copies, table, stage, cls, obs, gn, depth, keep, drive, state, flux, part, part_flux, band, gathered0, gathered1, chosen, sent, got,
    load_sem, halo_ss, halo_rs, fixed_ss, fixed_rs, ss1, rs1, ss2, rs2, self_sem,
):
    me, sp = lax.axis_index("dom"), lax.axis_index("space")
    gathered = (gathered0, gathered1)
    up, down = (sp + 7) % 8, (sp + 1) % 8

    loads = [
        pltpu.make_async_copy(classes, cls, load_sem.at[0]),
        pltpu.make_async_copy(particles, stage, load_sem.at[1]),
        pltpu.make_async_copy(gain, gn, load_sem.at[2]),
        pltpu.make_async_copy(observed, obs, load_sem.at[3]),
        pltpu.make_async_copy(table_in, table, load_sem.at[4]),
        pltpu.make_async_copy(copies_in, copies, load_sem.at[5]),
    ]
    for load in loads:
        load.start()

    barrier = pltpu.get_barrier_semaphore()

    @pl.loop(1, GROUP)
    def _(i):
        pl.semaphore_signal(barrier, inc=1, device_id=(peer_of(me, i), sp), device_id_type=MESH)

    for other in (up, down):
        pl.semaphore_signal(barrier, inc=1, device_id=(me, other), device_id_type=MESH)

    lane = lax.broadcasted_iota(jnp.int32, (8, 128), 1)
    sublane = lax.broadcasted_iota(jnp.int32, (8, 128), 0)

    row = lax.broadcasted_iota(jnp.int32, (512, 128), 0) % 256
    column = lax.broadcasted_iota(jnp.int32, (512, 128), 1)
    ahead = row - jnp.where(column < 64, column + 128, column)
    weights = jnp.where(ahead == 1, 8.0, 0.0) - jnp.where(ahead == -1, 8.0, 0.0)
    weights = weights - jnp.where(ahead == 2, 1.0, 0.0) + jnp.where(ahead == -2, 1.0, 0.0)
    band[...] = weights.astype(jnp.bfloat16)

    loads[0].wait()
    loads[4].wait()

    @pl.loop(0, TILES)
    def _(t):
        base = pl.multiple_of(t * 8, 8)
        for c in range(PANELS):
            kind = cls[pl.ds(base, 8), c * 128 : c * 128 + 128]
            d = jnp.zeros((8, 128), jnp.float32)
            for klass in range(CLASSES):
                d = jnp.where(kind == klass, table[klass], d)
            depth[c, pl.ds(base + PAD, 8), :] = d

    loads[1].wait()

    @pl.loop(0, 2 * TILES)
    def _(i):
        p, t = i // TILES, i % TILES
        base = pl.multiple_of(t * 8, 8)
        for c in range(PANELS):
            for f in range(3):
                v = stage[p, f, pl.ds(base, 8), c * 128 : c * 128 + 128]
                state[p, f, c, pl.ds(base + PAD, 8), :] = v
                if f == 2:
                    flux[p, c, pl.ds(base + PAD, 8), :] = depth[c, pl.ds(base + PAD, 8), :] * v

    none = jnp.zeros((8, 128), jnp.float32)

    @pl.loop(0, 4)
    def _(i):
        row = pl.multiple_of((i % 2) * 8 + (i // 2) * (ROWS + PAD), 8)
        for c in range(PANELS):
            drive[c, pl.ds(row, 8), :] = none
            for p in range(2):
                flux[p, c, pl.ds(row, 8), :] = none
                for f in range(3):
                    state[p, f, c, pl.ds(row, 8), :] = none
        for side in range(2):
            for p in range(2):
                for c in range(PANELS):
                    part_flux[side, p, c, pl.ds(pl.multiple_of(i * 8, 8), 8), :] = none
                    for f in range(3):
                        part[side, p, f, c, pl.ds(pl.multiple_of(i * 8, 8), 8), :] = none

    loads[2].wait()
    loads[3].wait()
    loads[5].wait()

    @pl.loop(0, TILES)
    def _(t):
        base = pl.multiple_of(t * 8, 8)
        for c in range(PANELS):
            g = gn[pl.ds(base, 8), c * 128 : c * 128 + 128]
            keep[c, pl.ds(base + PAD, 8), :] = 1.0 - g
            drive[c, pl.ds(base + PAD, 8), :] = g * obs[pl.ds(base, 8), c * 128 : c * 128 + 128]

    def shifts(panels):
        ahead = [pltpu.roll(v, 127, 1) for v in panels]
        ahead2 = [pltpu.roll(v, 126, 1) for v in panels]
        behind = [pltpu.roll(v, 1, 1) for v in panels]
        behind2 = [pltpu.roll(v, 2, 1) for v in panels]
        found = []
        for c in range(PANELS):
            nxt, prv = (c + 1) % PANELS, (c - 1) % PANELS
            found.append((
                jnp.where(lane < 127, ahead[c], ahead[nxt]),
                jnp.where(lane >= 1, behind[c], behind[prv]),
                jnp.where(lane < 126, ahead2[c], ahead2[nxt]),
                jnp.where(lane >= 2, behind2[c], behind2[prv]),
            ))
        return found

    def columns_of(panels):
        return [8.0 * (a - b) - (a2 - b2) for a, b, a2, b2 in shifts(panels)]

    def split_columns(panels):
        parts = []
        for c in range(PANELS):
            v = jnp.concatenate([panels[0][c], panels[1][c]], axis=0)
            high = v.astype(jnp.bfloat16)
            parts.append((high, (v - high.astype(jnp.float32)).astype(jnp.bfloat16)))
        rows = []
        for c in range(PANELS):
            here, ahead = parts[c], parts[(c + 1) % PANELS]
            rows.append(jnp.concatenate([here[0], ahead[0], here[1], ahead[1]], axis=1))
        product = jnp.dot(jnp.concatenate(rows, axis=0), band[...], preferred_element_type=jnp.float32)
        pieces = [product[16 * c : 16 * c + 16] for c in range(PANELS)]
        wide = lax.broadcasted_iota(jnp.int32, (16, 128), 1)
        found = [jnp.where(wide < 64, pieces[c - 1], pieces[c]) for c in range(PANELS)]
        return [v[:8] for v in found], [v[8:] for v in found]

    def all_columns(panels):
        if len(panels[0]) == 1:
            return [[columns_of(panels[p][0])] for p in range(2)]
        return [[columns_of(v) for v in panels[0]], split_columns(panels[1])]

    def put_heights(*windows):
        heres = [pl.ds(base + PAD, 8) for base, _, _ in windows]
        columns = all_columns(
            [[[depth[c, here, :] * state[p, 1, c, here, :] for c in range(PANELS)] for here in heres] for p in range(2)]
        )
        found = []
        for p in range(2):
            for w, (base, low, high) in enumerate(windows):
                inside = (base + sublane >= low) & (base + sublane < high)
                here = heres[w]
                for c, along in enumerate(columns[p][w]):
                    a = flux[p, c, pl.ds(base + PAD + 1, 8), :]
                    b = flux[p, c, pl.ds(base + PAD - 1, 8), :]
                    a2 = flux[p, c, pl.ds(base + PAD + 2, 8), :]
                    b2 = flux[p, c, pl.ds(base + PAD - 2, 8), :]
                    old = state[p, 0, c, here, :]
                    h = old - K * (along + (8.0 * (a - b) - (a2 - b2)))
                    h = keep[c, here, :] * h + drive[c, here, :]
                    found.append((p, c, here, jnp.where(inside, h, old)))
        for p, c, here, h in found:
            state[p, 0, c, here, :] = h

    def put_velocities(*bases):
        heres = [pl.ds(base + PAD, 8) for base in bases]
        columns = all_columns([[[state[p, 0, c, here, :] for c in range(PANELS)] for here in heres] for p in range(2)])
        found = []
        for p in range(2):
            for w, base in enumerate(bases):
                here = heres[w]
                for c, along in enumerate(columns[p][w]):
                    a = state[p, 0, c, pl.ds(base + PAD + 1, 8), :]
                    b = state[p, 0, c, pl.ds(base + PAD - 1, 8), :]
                    a2 = state[p, 0, c, pl.ds(base + PAD + 2, 8), :]
                    b2 = state[p, 0, c, pl.ds(base + PAD - 2, 8), :]
                    e, n = state[p, 1, c, here, :], state[p, 2, c, here, :]
                    e_new = e - K * along + (DT * F0) * n
                    n_new = n - K * (8.0 * (a - b) - (a2 - b2)) - (DT * F0) * e
                    found.append((p, c, here, e_new, n_new, depth[c, here, :] * n_new))
        for p, c, here, e, n, f in found:
            state[p, 1, c, here, :] = e
            state[p, 2, c, here, :] = n
            flux[p, c, here, :] = f

    def in_pairs(count, put, window):
        @pl.loop(0, count // 2)
        def _(i):
            put(window(i), window(i + count // 2))

        if count % 2:
            put(window(count - 1))

    def height_windows(count, window):
        in_pairs(count, put_heights, window)

    def velocity_windows(count, first):
        in_pairs(count, put_velocities, lambda i: first + 8 * i)

    def halo_copies(k):
        return [
            pltpu.make_async_remote_copy(
                src_ref=sent.at[k, side],
                dst_ref=got.at[k, 1 - side],
                send_sem=halo_ss.at[k, side],
                recv_sem=halo_rs.at[k, 1 - side],
                device_id=(me, other),
                device_id_type=MESH,
            )
            for side, other in enumerate((up, down))
        ]

    def send_halo(k):
        @pl.loop(0, 2)
        def _(side):
            base = pl.multiple_of(side * (ROWS - 8), 8)
            from_edge = sublane + side * (7 - 2 * sublane)
            for c in range(PANELS):
                f0, f1 = (flux[p, c, pl.ds(base + PAD, 8), :] for p in range(2))
                h0, h1 = (state[p, 0, c, pl.ds(base + PAD, 8), :] for p in range(2))
                second = jnp.where(side == 0, pltpu.roll(h0, 2, 0), pltpu.roll(h0, 6, 0))
                fourth = jnp.where(side == 0, pltpu.roll(h1, 6, 0), pltpu.roll(h1, 2, 0))
                sent[k, side, c, :, :] = jnp.where(
                    from_edge < 4,
                    jnp.where(from_edge < 2, f0, second),
                    jnp.where(from_edge < 6, pltpu.roll(f1, 4, 0), fourth),
                )

        for copy in halo_copies(k):
            copy.start()

    def inner(k):
        last = 8 - k

        def window(i):
            low = 4 * k - 2 + 8 * i
            return low - 4 * (i // last), low, ROWS + 2 - 4 * k

        height_windows(last + 1, window)
        velocity_windows(8 - k, 4 * k)

    def outer(k):
        @pl.loop(0, k)
        def _(i):
            put_heights(
                (8 * i - 4 * k, -PAD, 4 * k - 2), (ROWS - 4 * k + 8 * i, ROWS + 2 - 4 * k, ROWS + PAD)
            )

        send_halo(k - 1)

        @pl.loop(0, k)
        def _(i):
            put_velocities(8 * i - 4 * k, ROWS - 4 * k + 8 * i)

    def whole(k):
        height_windows(13 - k, lambda i: (4 * k - 18 + 8 * i, -PAD, 82 - 4 * k))
        send_halo(k - 1)
        velocity_windows(12 - k, 4 * k - 16)

    def other_part(k):
        for copy in halo_copies(k - 1):
            copy.wait_recv()
        third = k // 3
        for side in range(2):
            there = sp < 7 if side else sp > 0
            near = slice(24, 32) if side else slice(0, 8)
            for c in range(PANELS):
                message = jnp.where(there, got[k - 1, side, c, :, :], 0.0)
                for p in range(2):
                    part_flux[side, p, c, near, :] = pltpu.roll(message, 4, 0) if p else message
                    part[side, p, 0, c, near, :] = pltpu.roll(message, 2 if side == p else 6, 0)

        @pl.loop(0, 1 + third)
        def _(i):
            ats = (pl.multiple_of(8 + 8 * i, 8), pl.multiple_of(16 - 8 * i, 8))
            heres = [pl.ds(at, 8) for at in ats]
            owns = [pl.ds(pl.multiple_of(PAD - 8 + at + side * (ROWS - 16), 8), 8) for side, at in enumerate(ats)]
            columns = all_columns([
                [[depth[c, owns[side], :] * part[side, p, 1, c, heres[side], :] for c in range(PANELS)] for side in range(2)]
                for p in range(2)
            ])
            found = []
            for p in range(2):
                for side, at in enumerate(ats):
                    here, own = heres[side], owns[side]
                    for c, along in enumerate(columns[p][side]):
                        a = part_flux[side, p, c, pl.ds(at + 1, 8), :]
                        b = part_flux[side, p, c, pl.ds(at - 1, 8), :]
                        a2 = part_flux[side, p, c, pl.ds(at + 2, 8), :]
                        b2 = part_flux[side, p, c, pl.ds(at - 2, 8), :]
                        h = part[side, p, 0, c, here, :] - K * (along + (8.0 * (a - b) - (a2 - b2)))
                        found.append((side, p, c, here, keep[c, own, :] * h))
            for side, p, c, here, h in found:
                part[side, p, 0, c, here, :] = h

        @pl.loop(0, 1 + third)
        def _(i):
            ats = (pl.multiple_of(8 + 8 * i, 8), pl.multiple_of(16 - 8 * i, 8))
            heres = [pl.ds(at, 8) for at in ats]
            owns = [pl.ds(pl.multiple_of(PAD - 8 + at + side * (ROWS - 16), 8), 8) for side, at in enumerate(ats)]
            columns = all_columns([
                [[part[side, p, 0, c, heres[side], :] for c in range(PANELS)] for side in range(2)] for p in range(2)
            ])
            found = []
            for p in range(2):
                for side, at in enumerate(ats):
                    here, own = heres[side], owns[side]
                    for c, along in enumerate(columns[p][side]):
                        a = part[side, p, 0, c, pl.ds(at + 1, 8), :]
                        b = part[side, p, 0, c, pl.ds(at - 1, 8), :]
                        a2 = part[side, p, 0, c, pl.ds(at + 2, 8), :]
                        b2 = part[side, p, 0, c, pl.ds(at - 2, 8), :]
                        e, n = part[side, p, 1, c, here, :], part[side, p, 2, c, here, :]
                        e_new = e - K * along + (DT * F0) * n
                        n_new = n - K * (8.0 * (a - b) - (a2 - b2)) - (DT * F0) * e
                        found.append((side, p, c, here, e_new, n_new, depth[c, own, :] * n_new))
            for side, p, c, here, e, n, f in found:
                part[side, p, 1, c, here, :] = e
                part[side, p, 2, c, here, :] = n
                part_flux[side, p, c, here, :] = f

    def join():
        @pl.loop(0, 4)
        def _(j):
            side, i = j % 2, j // 2
            here = pl.ds(pl.multiple_of(8 + 8 * i, 8), 8)
            own = pl.ds(pl.multiple_of(PAD + 8 * i + side * (ROWS - 16), 8), 8)
            found = [
                (p, f, c, state[p, f, c, own, :] + part[side, p, f, c, here, :])
                for p in range(2) for f in range(3) for c in range(PANELS)
            ]
            for p, f, c, v in found:
                state[p, f, c, own, :] = v

    def own_collect(piece):
        return pltpu.make_async_copy(
            state.at[:, :, pl.ds(2 * quarter_of(me), 2), pl.ds(PAD + row_of(piece, me), 8), :],
            gathered[piece].at[pl.ds(2 * me, 2)],
            self_sem.at[piece],
        )

    def collect(piece, first=1, last=GROUP):
        @pl.loop(first, last)
        def _(i):
            d = peer_of(me, i)
            pltpu.make_async_remote_copy(
                src_ref=state.at[:, :, pl.ds(2 * quarter_of(d), 2), pl.ds(PAD + row_of(piece, d), 8), :],
                dst_ref=gathered[piece].at[pl.ds(2 * me, 2)],
                send_sem=ss1.at[piece],
                recv_sem=rs1.at[piece],
                device_id=(d, sp),
                device_id_type=MESH,
            ).start()

        if last == GROUP:
            own_collect(piece).start()

    def own_deliver(piece):
        return pltpu.make_async_copy(
            chosen.at[piece, pl.ds(2 * me, 2)],
            out.at[:, :, pl.ds(row_of(piece, me), 8), pl.ds(256 * quarter_of(me), 256)],
            self_sem.at[2 + piece],
        )

    def all_of(piece, sem):
        whole = gathered[piece].at[pl.ds(0, 30)]
        return pltpu.make_async_copy(whole, whole, sem.at[piece])

    def deliver(piece):
        all_of(piece, rs1).wait()
        own_collect(piece).wait()

        def pick(d):
            sources = [copies[2 * d + slot] for slot in range(2)]
            picked = [gathered[piece][source, f, c] for source in sources for f in range(3) for c in range(2)]
            for n, v in enumerate(picked):
                f, c = n // 2 % 3, n % 2
                chosen[piece, 2 * d + n // 6, f, :, c * 128 : c * 128 + 128] = v

        @pl.loop(1, GROUP)
        def _(i):
            d = peer_of(me, i)
            pick(d)
            pltpu.make_async_remote_copy(
                src_ref=chosen.at[piece, pl.ds(2 * d, 2)],
                dst_ref=out.at[:, :, pl.ds(row_of(piece, me), 8), pl.ds(256 * quarter_of(me), 256)],
                send_sem=ss2.at[piece],
                recv_sem=rs2.at[piece],
                device_id=(d, sp),
                device_id_type=MESH,
            ).start()

        pick(me)
        own_deliver(piece).start()

    fixed = [
        pltpu.make_async_remote_copy(
            src_ref=ref.at[:, pl.ds(source, 8), :],
            dst_ref=ref.at[:, pl.ds(target, 8), :],
            send_sem=fixed_ss.at[n, side],
            recv_sem=fixed_rs.at[n, 1 - side],
            device_id=(me, other),
            device_id_type=MESH,
        )
        for n, ref in enumerate((depth, keep))
        for side, other, source, target in ((0, up, PAD, PAD + ROWS), (1, down, PAD + ROWS - 8, PAD - 8))
    ]

    def take_fixed():
        for copy in fixed:
            copy.wait_recv()
        for there, row in ((sp > 0, PAD - 8), (sp < 7, PAD + ROWS)):
            for ref in (depth, keep):
                for c in range(PANELS):
                    ref[c, row : row + 8, :] = jnp.where(there, ref[c, row : row + 8, :], 0.0)

    pl.semaphore_wait(barrier, GROUP + 1)
    for copy in fixed:
        copy.start()
    inner(1)
    inner(2)
    take_fixed()
    outer(1)
    outer(2)
    whole(3)
    whole(4)
    collect(0)

    @pl.loop(1, STEPS + 1)
    def _(k):
        other_part(k)

    join()
    collect(1)
    deliver(0)
    deliver(1)
    for piece in range(2):
        all_of(piece, rs2).wait()
        own_deliver(piece).wait()
    for piece in range(2):
        all_of(piece, ss1).wait()
        all_of(piece, ss2).wait()
    for copy in fixed:
        copy.wait_send()

    @pl.loop(0, STEPS)
    def _(k):
        for copy in halo_copies(k):
            copy.wait_send()


def shards(particles, copies, depth_class, depth_table, observed, nudge_gain):
    f32 = jnp.float32
    sem = pltpu.SemaphoreType.DMA
    anywhere = pl.BlockSpec(memory_space=pl.ANY)
    return pl.pallas_call(
        kernel,
        out_shape=jax.ShapeDtypeStruct(particles.shape, f32),
        in_specs=[anywhere] * 6,
        out_specs=anywhere,
        scratch_shapes=[
            pltpu.SMEM((32,), jnp.int32),
            pltpu.SMEM((CLASSES,), f32),
            pltpu.VMEM((2, 3, ROWS, 1024), f32),
            pltpu.VMEM((ROWS, 1024), jnp.int32),
            pltpu.VMEM((ROWS, 1024), f32),
            pltpu.VMEM((ROWS, 1024), f32),
            pltpu.VMEM((PANELS, ROWS + 2 * PAD, 128), f32),
            pltpu.VMEM((PANELS, ROWS + 2 * PAD, 128), f32),
            pltpu.VMEM((PANELS, ROWS + 2 * PAD, 128), f32),
            pltpu.VMEM((2, 3, PANELS, ROWS + 2 * PAD, 128), f32),
            pltpu.VMEM((2, PANELS, ROWS + 2 * PAD, 128), f32),
            pltpu.VMEM((2, 2, 3, PANELS, 32, 128), f32),
            pltpu.VMEM((2, 2, PANELS, 32, 128), f32),
            pltpu.VMEM((512, 128), jnp.bfloat16),
            pltpu.VMEM((32, 3, 2, 8, 128), f32),
            pltpu.VMEM((32, 3, 2, 8, 128), f32),
            pltpu.VMEM((2, 32, 3, 8, 256), f32),
            pltpu.VMEM((STEPS, 2, PANELS, 8, 128), f32),
            pltpu.VMEM((STEPS, 2, PANELS, 8, 128), f32),
            sem((6,)), sem((STEPS, 2)), sem((STEPS, 2)), sem((2, 2)), sem((2, 2)),
            sem((2,)), sem((2,)), sem((2,)), sem((2,)), sem((4,)),
        ],
        compiler_params=pltpu.CompilerParams(
            collective_id=0, has_side_effects=True, vmem_limit_bytes=60 * 2**20
        ),
    )(copies, depth_table, particles, depth_class, observed, nudge_gain)


def solution(mesh):
    placed = (
        P("dom", None, "space", None),
        P(),
        P("space", None),
        P(),
        P("space", None),
        P("space", None),
    )
    return jax.shard_map(
        shards, mesh=mesh, in_specs=placed, out_specs=P("dom", None, "space", None), check_vma=False
    )
```
